256 devices in a mesh: seq: 32 (over z, y_hi, core), tp: 8 (over x, y_lo).
Axes of the slice: x: 4, y: 4 (y_hi: 2, y_lo: 2; y = y_hi * 2 + y_lo), z: 8, core: 2. Of those that a mesh axis runs over, the one named last changes fastest.
Arguments:
- queries: bfloat16 [8192, 8192], P('seq', 'tp'), may hold values from -128 to 128
- keys: bfloat16 [8192, 1024], P('seq', 'tp'), may hold values from -4 to 4
- values: bfloat16 [8192, 1024], P('seq', 'tp'), may hold values from -4 to 4
- out_weight: bfloat16 [8192, 4096], P('tp'), may hold values from -0.25 to 0.25
- step_queries: bfloat16 [32, 8192], P('seq', 'tp'), may hold values from -128 to 128
- new_keys: bfloat16 [32, 1024], P('seq', 'tp'), may hold values from -4 to 4
- new_values: bfloat16 [32, 1024], P('seq', 'tp'), may hold values from -4 to 4
- key_cache: bfloat16 [32, 4096, 1024], P('seq', None, 'tp'), may hold values from -4 to 4
- value_cache: bfloat16 [32, 4096, 1024], P('seq', None, 'tp'), may hold values from -4 to 4
- cache_lens: int32 [32], P('seq'), may hold values from 2 to 4096
Outputs:
- prefill_out: bfloat16 [8192, 4096], P(('seq', 'tp'))
- decode_out: bfloat16 [32, 4096], P('seq', 'tp')
The draws below stay inside these ranges and needn't reach their ends.
All inputs are finite; a program needn't handle non-finite values.
Results may differ from the reference program's by a relative error of at most 0.019.
Values may be sent and summed in bfloat16 or wider, within the bound.
No kernel may reach another device: no remote copies, remote signals or barrier semaphores. Data moves between devices by JAX's collectives and lax.ppermute only.
A program may use at most 192 MiB of HBM per device.

```python
import jax
import jax.numpy as jnp
from jax import lax

D = 4096
HEAD = 128
HEADS = 64
KV_HEADS = 8
CACHE = 4096
TOKENS = 8192
REQUESTS = 32
N_TP = 8


def shared_keys(key):
    return jnp.clip(jax.random.normal(key, (TOKENS, KV_HEADS * HEAD), jnp.float32), -4.0, 4.0)


def shared_cache(key):
    return jnp.clip(jax.random.normal(key, (REQUESTS, CACHE, KV_HEADS * HEAD), jnp.float32), -4.0, 4.0)


def shared_fresh(key):
    return jnp.clip(jax.random.normal(jax.random.fold_in(key, 91), (REQUESTS, KV_HEADS * HEAD), jnp.float32), -4.0, 4.0)


def spread_heads(rows):
    count = rows.shape[0]
    return jnp.repeat(rows.reshape(count, KV_HEADS, 1, HEAD), HEADS // KV_HEADS, axis=2).reshape(count, HEADS * HEAD)


def draw_keys(key, part):
    base = shared_keys(key)
    return base.astype(jnp.bfloat16)


def draw_queries(key, part):
    key = jax.random.fold_in(key, 5)
    fresh = jnp.clip(1.5 * jax.random.normal(key, (TOKENS, HEADS * HEAD), jnp.float32), -6.0, 6.0)
    return fresh.astype(jnp.bfloat16)


def draw_key_cache(key, part):
    base = shared_cache(key)
    return base.astype(jnp.bfloat16)


def draw_new_keys(key, part):
    fresh_rows = shared_fresh(key)
    return fresh_rows.astype(jnp.bfloat16)


def draw_step_queries(key, part):
    fresh_rows = shared_fresh(key)
    key = jax.random.fold_in(key, 11)
    drawn = jnp.clip(jax.random.normal(key, (REQUESTS, HEADS * HEAD), jnp.float32), -4.0, 4.0)
    drawn = drawn + 0.6 * spread_heads(fresh_rows)
    return drawn.astype(jnp.bfloat16)


def draw_cache_lens(key, part):
    key = jax.random.fold_in(key, 13)
    drawn = jax.random.randint(key, (REQUESTS,), 2, CACHE + 1)
    chosen = jax.random.randint(jax.random.fold_in(key, 1), (), 0, REQUESTS)
    return jnp.where(jnp.arange(REQUESTS) == chosen, CACHE, drawn).astype(jnp.int32)


def levels(rng, dims, split, least, high):
    def one(position, blocks):
        steps = jax.random.uniform(jax.random.fold_in(jax.random.fold_in(rng, 6), position), (blocks,), jnp.float32, least / len(split), high / len(split))
        return jnp.repeat(jnp.exp(steps), dims[position] // blocks).reshape((-1,) + (1,) * (len(dims) - position - 1))

    level = one(*split[0])
    for cut in split[1:]:
        level = level * one(*cut)
    return level


def normal_values(rng, shape, deviation, most, shards=(), kind=jnp.bfloat16):
    loudness = levels(rng, shape, shards, -0.22, 0.18) if shards else 1.0
    entries = jax.random.normal(rng, shape, jnp.float32) * deviation * loudness
    return jnp.minimum(jnp.maximum(entries, -most), most).astype(kind)


def setup_inputs(seed: int = 0) -> dict:
    seeds = jax.random.split(jax.random.key(seed), 11)
    queries = draw_queries(jax.random.fold_in(seeds[10], 71), 0)
    keys = draw_keys(jax.random.fold_in(seeds[10], 71), 0)
    values = normal_values(seeds[2], (TOKENS, KV_HEADS * HEAD), 1.0, 4.0, ((0, 32), (1, 8)))
    out_weight = normal_values(seeds[3], (HEADS * HEAD, D), (HEADS * HEAD // 16) ** -0.5, 0.25, ((0, 8),))
    step_queries = draw_step_queries(jax.random.fold_in(seeds[10], 71), 0)
    new_keys = draw_new_keys(jax.random.fold_in(seeds[10], 71), 0)
    new_values = normal_values(seeds[6], (REQUESTS, KV_HEADS * HEAD), 1.0, 4.0, ((0, 32), (1, 8)))
    key_cache = draw_key_cache(jax.random.fold_in(seeds[10], 71), 0)
    value_cache = normal_values(seeds[8], (REQUESTS, CACHE, KV_HEADS * HEAD), 1.0, 4.0, ((0, 32), (2, 8)))
    cache_lens = draw_cache_lens(jax.random.fold_in(seeds[10], 71), 0)
    return {"queries": queries, "keys": keys, "values": values, "out_weight": out_weight, "step_queries": step_queries, "new_keys": new_keys, "new_values": new_values, "key_cache": key_cache, "value_cache": value_cache, "cache_lens": cache_lens}


neg_large = -1e30


def twice_round(values_in):
    return lax.optimization_barrier(values_in.astype(jnp.bfloat16)).astype(jnp.float32)


def group_sum(attention, out_weight):
    width = HEADS * HEAD // N_TP
    summed = jnp.zeros((attention.shape[0], D), jnp.float32)
    for group_index in range(N_TP):
        left = attention[:, group_index * width:(group_index + 1) * width].astype(jnp.float32)
        right = out_weight[group_index * width:(group_index + 1) * width].astype(jnp.float32)
        part = jnp.dot(left, right, precision=lax.Precision.HIGHEST)
        summed = summed + twice_round(part)
    return summed.astype(jnp.bfloat16)


def reference(queries, keys, values, out_weight, step_queries, new_keys, new_values, key_cache, value_cache, cache_lens):
    group_size = HEADS // KV_HEADS
    score_scale = HEAD ** -0.5
    positions = jnp.arange(TOKENS)
    causal = positions[:, None] >= positions[None, :]

    def one_head(head_index):
        kv_index = head_index // group_size
        query_rows = lax.dynamic_slice_in_dim(queries, head_index * HEAD, HEAD, 1).astype(jnp.float32)
        key_rows = lax.dynamic_slice_in_dim(keys, kv_index * HEAD, HEAD, 1).astype(jnp.float32)
        value_rows = lax.dynamic_slice_in_dim(values, kv_index * HEAD, HEAD, 1).astype(jnp.float32)
        scores = jnp.dot(query_rows, key_rows.T, precision=lax.Precision.HIGHEST) * score_scale
        row_peak = jnp.max(jnp.where(causal, scores, neg_large), axis=1, keepdims=True)
        weights = jnp.where(causal, jnp.exp(scores - row_peak), 0.0)
        row_total = jnp.sum(weights, axis=1, keepdims=True)
        rounded = twice_round(weights)
        return jnp.dot(rounded, value_rows, precision=lax.Precision.HIGHEST) / row_total

    head_outputs = lax.map(one_head, jnp.arange(HEADS, dtype=jnp.int32))
    attention = head_outputs.transpose(1, 0, 2).reshape(TOKENS, HEADS * HEAD).astype(jnp.bfloat16)
    prefill_out = group_sum(attention, out_weight)

    step_rows = step_queries.astype(jnp.float32).reshape(REQUESTS, KV_HEADS, group_size, HEAD)
    cache_keys = key_cache.astype(jnp.float32).reshape(REQUESTS, CACHE, KV_HEADS, HEAD)
    cache_values = value_cache.astype(jnp.float32).reshape(REQUESTS, CACHE, KV_HEADS, HEAD)
    fresh_keys = new_keys.astype(jnp.float32).reshape(REQUESTS, KV_HEADS, HEAD)
    fresh_values = new_values.astype(jnp.float32).reshape(REQUESTS, KV_HEADS, HEAD)
    cached_scores = jnp.einsum("rkgd,rckd->rkgc", step_rows, cache_keys, precision=lax.Precision.HIGHEST) * score_scale
    own_score = jnp.einsum("rkgd,rkd->rkg", step_rows, fresh_keys, precision=lax.Precision.HIGHEST) * score_scale
    cached_live = (jnp.arange(CACHE, dtype=jnp.int32)[None, :] < cache_lens[:, None])[:, None, None, :]
    step_peak = jnp.maximum(jnp.max(jnp.where(cached_live, cached_scores, neg_large), axis=-1), own_score)
    cached_weights = jnp.where(cached_live, jnp.exp(cached_scores - step_peak[..., None]), 0.0)
    own_weight = jnp.exp(own_score - step_peak)
    step_total = jnp.sum(cached_weights, axis=-1) + own_weight
    mixed = jnp.einsum("rkgc,rckd->rkgd", twice_round(cached_weights), cache_values, precision=lax.Precision.HIGHEST)
    mixed = mixed + twice_round(own_weight)[..., None] * fresh_values[:, :, None, :]
    step_attention = (mixed / step_total[..., None]).reshape(REQUESTS, HEADS * HEAD).astype(jnp.bfloat16)
    decode_out = group_sum(step_attention, out_weight)
    return prefill_out, decode_out
```

```python
import functools
import math

import jax
import jax.numpy as jnp
from jax import lax
from jax.experimental import pallas as pl
from jax.experimental.pallas import tpu as pltpu
from jax.sharding import PartitionSpec as P

HEAD = 128
SCALE = HEAD ** -0.5 * math.log2(math.e)
LOW = -1e30
NT = (((1,), (1,)), ((), ()))
Z, YH, CORE = 8, 2, 2


def seq_pairs(move):
    pairs = []
    for z in range(Z):
        for yh in range(YH):
            for c in range(CORE):
                z2, yh2, c2 = move(z, yh, c)
                pairs.append(((z * YH + yh) * CORE + c, ((z2 % Z) * YH + yh2) * CORE + c2))
    return pairs


SWAP_Y = seq_pairs(lambda z, yh, c: (z, 1 - yh, c))
SWAP_CORE = seq_pairs(lambda z, yh, c: (z, yh, 1 - c))
RING = seq_pairs(lambda z, yh, c: (z + 1 if c == 0 else z - 1, yh, c))


def split_queries(q_ref, q2_ref, rows, heads):
    for h in range(heads):
        scaled = q_ref[:, h * HEAD:(h + 1) * HEAD].astype(jnp.float32) * SCALE
        high = scaled.astype(jnp.bfloat16)
        low = (scaled - high.astype(jnp.float32)).astype(jnp.bfloat16)
        q2_ref[h * rows:(h + 1) * rows, :HEAD] = high
        q2_ref[h * rows:(h + 1) * rows, HEAD:] = low


def spread(src_ref, k2_ref, v2_ref, at, blocks, rows):
    for b in range(blocks):
        k = src_ref[2 * b * rows:(2 * b + 1) * rows, :]
        v = src_ref[(2 * b + 1) * rows:(2 * b + 2) * rows, :]
        here = slice(at + b * rows, at + (b + 1) * rows)
        k2_ref[here, :HEAD] = k
        k2_ref[here, HEAD:] = k
        v2_ref[here, :HEAD] = v
        v2_ref[here, HEAD:] = jnp.ones_like(v)


def attend(q2_ref, k2_ref, v2_ref, lo, hi, m_ref, acc_ref, m_out, acc_out, rows, heads, mask=None):
    first = m_ref is None
    for h in range(heads):
        part = slice(h * rows, (h + 1) * rows)
        s = lax.dot_general(q2_ref[part, :], k2_ref[lo:hi, :], NT, preferred_element_type=jnp.float32)
        if mask is not None:
            s = jnp.where(mask, s, LOW)
        peak = jnp.max(s, axis=1, keepdims=True)
        if not first:
            old = m_ref[part, :1]
            peak = jnp.maximum(old, peak)
        p = jnp.exp2(s - peak).astype(jnp.bfloat16)
        mixed = jnp.dot(p, v2_ref[lo:hi, :], preferred_element_type=jnp.float32)
        if not first:
            mixed = mixed + acc_ref[part, :] * jnp.exp2(old - peak)
        acc_out[part, :] = mixed
        m_out[part, :] = jnp.broadcast_to(peak, (rows, HEAD))


def local_kernel(edge_ref, q_ref, kv_ref, q2_ref, m_ref, acc_ref, k2_ref, v2_ref, *, rows, heads):
    split_queries(q_ref, q2_ref, rows, heads)
    spread(kv_ref, k2_ref, v2_ref, 0, 4, rows)
    row = lax.broadcasted_iota(jnp.int32, (rows, rows), 0)
    col = lax.broadcasted_iota(jnp.int32, (rows, rows), 1)
    mask = jnp.concatenate([(row - col) >= edge_ref[b] for b in range(4)], axis=1)
    attend(q2_ref, k2_ref, v2_ref, 0, 4 * rows, None, None, m_ref, acc_ref, rows, heads, mask)


def step_kernel(live_ref, q2_ref, a_ref, b_ref, m_in, acc_in, m_ref, acc_ref, k2_ref, v2_ref, *, rows, heads):
    n = 4 * rows
    both = jnp.logical_and(live_ref[0] == 1, live_ref[1] == 1)
    one = jnp.logical_xor(live_ref[0] == 1, live_ref[1] == 1)

    @pl.when(both)
    def _():
        spread(a_ref, k2_ref, v2_ref, 0, 4, rows)
        spread(b_ref, k2_ref, v2_ref, n, 4, rows)
        attend(q2_ref, k2_ref, v2_ref, 0, 2 * n, m_in, acc_in, m_ref, acc_ref, rows, heads)

    @pl.when(one)
    def _():
        @pl.when(live_ref[0] == 1)
        def _():
            spread(a_ref, k2_ref, v2_ref, 0, 4, rows)

        @pl.when(live_ref[1] == 1)
        def _():
            spread(b_ref, k2_ref, v2_ref, 0, 4, rows)

        attend(q2_ref, k2_ref, v2_ref, 0, n, m_in, acc_in, m_ref, acc_ref, rows, heads)

    @pl.when(jnp.logical_and(live_ref[0] == 0, live_ref[1] == 0))
    def _():
        m_ref[...] = m_in[...]
        acc_ref[...] = acc_in[...]


def last_kernel(live_ref, q2_ref, a_ref, b_ref, m_in, acc_in, w_hbm, out_ref, w_ref, att_ref, acc_ref, m_ref,
                k2_ref, v2_ref, sem, *, rows, heads, n_tp):
    fetch = pltpu.make_async_copy(w_hbm, w_ref, sem)
    fetch.start()
    n = 4 * rows

    @pl.when(live_ref[0] == 1)
    def _():
        spread(a_ref, k2_ref, v2_ref, 0, 2, rows)
        spread(b_ref, k2_ref, v2_ref, 2 * rows, 2, rows)
        attend(q2_ref, k2_ref, v2_ref, 0, n, m_in, acc_in, m_ref, acc_ref, rows, heads)

    @pl.when(live_ref[0] == 0)
    def _():
        acc_ref[...] = acc_in[...]

    for h in range(heads):
        acc = acc_ref[h * rows:(h + 1) * rows, :]
        att_ref[:, h * HEAD:(h + 1) * HEAD] = (acc[:, :HEAD] / acc[:, HEAD:]).astype(jnp.bfloat16)
    fetch.wait()
    wide = w_ref.shape[1] // 4
    for g in range(4):
        part = jnp.dot(att_ref[...], w_ref[:, g * wide:(g + 1) * wide], preferred_element_type=jnp.float32)
        out_ref[:, :, g * wide:(g + 1) * wide] = part.astype(jnp.bfloat16).reshape(n_tp, rows // n_tp, wide)


def body(queries, keys, values, out_weight, step_queries, new_keys, new_values, key_cache, value_cache, cache_lens):
    rows = queries.shape[0]
    heads = queries.shape[1] // HEAD
    n_tp = lax.axis_size("tp")
    width = out_weight.shape[1]
    seq = lax.axis_index("seq")
    z, yh, core = seq // (YH * CORE), seq // CORE % YH, seq % CORE

    own = jnp.concatenate([keys, values], axis=0)
    pair = jnp.concatenate([own, lax.ppermute(own, "seq", SWAP_Y)], axis=0)
    here = jnp.concatenate([pair, lax.ppermute(pair, "seq", SWAP_CORE)], axis=0)
    ring = [here]
    for k in range(1, 4):
        ring.append(lax.ppermute(ring[-1], "seq", RING))
    ring.append(lax.ppermute(ring[-1][: here.shape[0] // 2], "seq", RING))
    other = [None] + [lax.ppermute(block, "seq", SWAP_CORE) for block in ring[1:]]

    vmem = pl.BlockSpec(memory_space=pltpu.VMEM)
    smem = pl.BlockSpec(memory_space=pltpu.SMEM)
    state = (
        jax.ShapeDtypeStruct((heads * rows, HEAD), jnp.float32),
        jax.ShapeDtypeStruct((heads * rows, 2 * HEAD), jnp.float32),
    )
    all_seen, none_seen = -rows, rows
    edges = jnp.stack([
        jnp.int32(0),
        jnp.where(yh == 1, all_seen, none_seen),
        jnp.where(core == 1, all_seen, none_seen),
        jnp.where(yh == 1, all_seen, none_seen),
    ]).astype(jnp.int32)
    params = pltpu.CompilerParams(vmem_limit_bytes=36 * 2**20)

    def cost(keys_seen, extra_flops=0, extra_bytes=0):
        return pl.CostEstimate(
            flops=4 * heads * rows * keys_seen * 256 + extra_flops,
            bytes_accessed=2 * 2**20 + extra_bytes,
            transcendentals=heads * rows * keys_seen,
        )

    q2, m, acc = pl.pallas_call(
        functools.partial(local_kernel, rows=rows, heads=heads),
        in_specs=[smem, vmem, vmem],
        out_specs=[vmem] * 3,
        out_shape=(jax.ShapeDtypeStruct((heads * rows, 2 * HEAD), jnp.bfloat16),) + state,
        scratch_shapes=[pltpu.VMEM((4 * rows, 2 * HEAD), jnp.bfloat16)] * 2,
        compiler_params=params,
        cost_estimate=cost(4 * rows),
        name="attend_local",
    )(edges, queries, here)
    for k in range(1, 4):
        up, down = z >= k, z + k >= Z
        live = jnp.stack([jnp.where(core == 0, up, down), jnp.where(core == 0, down, up)]).astype(jnp.int32)
        m, acc = pl.pallas_call(
            functools.partial(step_kernel, rows=rows, heads=heads),
            in_specs=[smem] + [vmem] * 5,
            out_specs=[vmem] * 2,
            out_shape=state,
            input_output_aliases={4: 0, 5: 1},
            scratch_shapes=[pltpu.VMEM((8 * rows, 2 * HEAD), jnp.bfloat16)] * 2,
            compiler_params=params,
            cost_estimate=cost(8 * rows),
            name=f"attend_{k}",
        )(live, q2, ring[k], other[k], m, acc)
    live = (z >= 4).astype(jnp.int32).reshape(1)
    partial = pl.pallas_call(
        functools.partial(last_kernel, rows=rows, heads=heads, n_tp=n_tp),
        in_specs=[smem] + [vmem] * 5 + [pl.BlockSpec(memory_space=pl.ANY)],
        out_specs=vmem,
        out_shape=jax.ShapeDtypeStruct((n_tp, rows // n_tp, width), jnp.bfloat16),
        scratch_shapes=[
            pltpu.VMEM(out_weight.shape, jnp.bfloat16),
            pltpu.VMEM((rows, heads * HEAD), jnp.bfloat16),
            pltpu.VMEM(state[1].shape, jnp.float32),
            pltpu.VMEM(state[0].shape, jnp.float32),
            pltpu.VMEM((4 * rows, 2 * HEAD), jnp.bfloat16),
            pltpu.VMEM((4 * rows, 2 * HEAD), jnp.bfloat16),
            pltpu.SemaphoreType.DMA,
        ],
        compiler_params=params,
        cost_estimate=cost(4 * rows, 2 * rows * heads * HEAD * width, 10 * 2**20),
        name="attend_project",
    )(live, q2, ring[4], other[4], m, acc, out_weight)
    swapped = lax.all_to_all(partial, "tp", 0, 0)
    prefill_out = jnp.sum(swapped.astype(jnp.float32), axis=0).astype(jnp.bfloat16)

    request_count = step_queries.shape[0]
    kv_local = keys.shape[1] // HEAD
    group_size = heads // kv_local
    cache_rows = key_cache.shape[1]
    score_scale = HEAD ** -0.5
    step_rows = step_queries.reshape(request_count, kv_local, group_size, HEAD)
    cache_keys = key_cache.reshape(request_count, cache_rows, kv_local, HEAD)
    cache_values = value_cache.reshape(request_count, cache_rows, kv_local, HEAD)
    fresh_keys = new_keys.reshape(request_count, kv_local, HEAD)
    fresh_values = new_values.reshape(request_count, kv_local, HEAD)
    cached_scores = jnp.einsum(
        "rkgd,rckd->rkgc", step_rows, cache_keys, preferred_element_type=jnp.float32) * score_scale
    own_score = jnp.einsum("rkgd,rkd->rkg", step_rows, fresh_keys, preferred_element_type=jnp.float32) * score_scale
    cached_live = (jnp.arange(cache_rows, dtype=jnp.int32)[None, :] < cache_lens[:, None])[:, None, None, :]
    step_peak = jnp.maximum(jnp.max(jnp.where(cached_live, cached_scores, LOW), axis=-1), own_score)
    cached_weights = jnp.where(cached_live, jnp.exp(cached_scores - step_peak[..., None]), 0.0)
    own_weight = jnp.exp(own_score - step_peak)
    step_total = jnp.sum(cached_weights, axis=-1) + own_weight
    mixed = jnp.einsum(
        "rkgc,rckd->rkgd", cached_weights.astype(jnp.bfloat16), cache_values, preferred_element_type=jnp.float32)
    own_rounded = own_weight.astype(jnp.bfloat16).astype(jnp.float32)
    mixed = mixed + own_rounded[..., None] * fresh_values.astype(jnp.float32)[:, :, None, :]
    step_attention = (mixed / step_total[..., None]).reshape(request_count, heads * HEAD).astype(jnp.bfloat16)
    step_partial = jnp.dot(step_attention, out_weight, preferred_element_type=jnp.float32)
    decode_out = lax.psum_scatter(step_partial.astype(jnp.bfloat16), "tp", scatter_dimension=1, tiled=True)
    return prefill_out, decode_out


def solution(mesh):
    return jax.shard_map(
        body,
        mesh=mesh,
        in_specs=(
            P("seq", "tp"),
            P("seq", "tp"),
            P("seq", "tp"),
            P("tp", None),
            P("seq", "tp"),
            P("seq", "tp"),
            P("seq", "tp"),
            P("seq", None, "tp"),
            P("seq", None, "tp"),
            P("seq"),
        ),
        out_specs=(P(("seq", "tp"), None), P("seq", "tp")),
        check_vma=False,
    )
```

```python
import functools
import math

import jax
import jax.numpy as jnp
from jax import lax
from jax.experimental import pallas as pl
from jax.experimental.pallas import tpu as pltpu
from jax.sharding import PartitionSpec as P

HEAD = 128
SCALE = HEAD ** -0.5 * math.log2(math.e)
LOW = -1e30
STEP_ROWS = 16
STEP_ROWS = 16
NT = (((1,), (1,)), ((), ()))
EDGES, AFAR, OWN, OTHER = 0, 4, 4, 7
Z, YH, CORE = 8, 2, 2


def seq_pairs(move):
    pairs = []
    for z in range(Z):
        for yh in range(YH):
            for c in range(CORE):
                z2, yh2, c2 = move(z, yh, c)
                pairs.append(((z * YH + yh) * CORE + c, ((z2 % Z) * YH + yh2) * CORE + c2))
    return pairs


SWAP_Y = seq_pairs(lambda z, yh, c: (z, 1 - yh, c))
SWAP_CORE = seq_pairs(lambda z, yh, c: (z, yh, 1 - c))
SWAP_BOTH = seq_pairs(lambda z, yh, c: (z, 1 - yh, 1 - c))
FAR = seq_pairs(lambda z, yh, c: (z + Z // 2, yh, c))
RING = seq_pairs(lambda z, yh, c: (z + 1 if c == 0 else z - 1, yh, c))


def split_queries(q_ref, q2_ref, rows, heads):
    for h in range(heads):
        scaled = q_ref[:, h * HEAD:(h + 1) * HEAD].astype(jnp.float32) * SCALE
        high = scaled.astype(jnp.bfloat16)
        low = (scaled - high.astype(jnp.float32)).astype(jnp.bfloat16)
        q2_ref[h * rows:(h + 1) * rows, :HEAD] = high
        q2_ref[h * rows:(h + 1) * rows, HEAD:] = low


def spread(sources, k2_ref, v2_ref, at, rows):
    for src in sources:
        for b in range(src.shape[0] // (2 * rows)):
            k = src[2 * b * rows:(2 * b + 1) * rows, :]
            v = src[(2 * b + 1) * rows:(2 * b + 2) * rows, :]
            k2_ref[at:at + rows, :HEAD] = k
            k2_ref[at:at + rows, HEAD:] = k
            v2_ref[at:at + rows, :HEAD] = v
            v2_ref[at:at + rows, HEAD:] = jnp.ones_like(v)
            at += rows


def attend(q2_ref, k2_ref, v2_ref, n, m_ref, acc_ref, m_out, acc_out, rows, heads, mask=None):
    first = m_ref is None
    for h in range(heads):
        part = slice(h * rows, (h + 1) * rows)
        s = lax.dot_general(q2_ref[part, :], k2_ref[:n, :], NT, preferred_element_type=jnp.float32)
        if mask is not None:
            s = jnp.where(mask, s, LOW)
        peak = jnp.max(s, axis=1, keepdims=True)
        if not first:
            old = m_ref[part, :1]
            peak = jnp.maximum(old, peak)
        p = jnp.exp2(s - peak).astype(jnp.bfloat16)
        mixed = jnp.dot(p, v2_ref[:n, :], preferred_element_type=jnp.float32)
        if not first:
            mixed = mixed + acc_ref[part, :] * jnp.exp2(old - peak)
        acc_out[part, :] = mixed
        m_out[part, :] = jnp.broadcast_to(peak, (rows, HEAD))


def local_kernel(flag_ref, q_ref, kv_ref, q2_ref, m_ref, acc_ref, k2_ref, v2_ref, *, rows, heads):
    split_queries(q_ref, q2_ref, rows, heads)
    spread([kv_ref], k2_ref, v2_ref, 0, rows)
    row = lax.broadcasted_iota(jnp.int32, (rows, rows), 0)
    col = lax.broadcasted_iota(jnp.int32, (rows, rows), 1)
    mask = jnp.concatenate([(row - col) >= flag_ref[EDGES + b] for b in range(4)], axis=1)
    attend(q2_ref, k2_ref, v2_ref, 4 * rows, None, None, m_ref, acc_ref, rows, heads, mask)


def step_kernel(flag_ref, q2_ref, *refs, rows, heads, counts, at):
    a, b = refs[:counts[0]], refs[counts[0]:sum(counts)]
    m_in, acc_in, m_ref, acc_ref, k2_ref, v2_ref = refs[sum(counts):]
    n = 4 * rows
    a_live, b_live = flag_ref[at[0]] == 1, flag_ref[at[1]] == 1

    @pl.when(jnp.logical_and(a_live, b_live))
    def _():
        spread(a, k2_ref, v2_ref, 0, rows)
        spread(b, k2_ref, v2_ref, n, rows)
        attend(q2_ref, k2_ref, v2_ref, 2 * n, m_in, acc_in, m_ref, acc_ref, rows, heads)

    @pl.when(jnp.logical_xor(a_live, b_live))
    def _():
        @pl.when(a_live)
        def _():
            spread(a, k2_ref, v2_ref, 0, rows)

        @pl.when(b_live)
        def _():
            spread(b, k2_ref, v2_ref, 0, rows)

        attend(q2_ref, k2_ref, v2_ref, n, m_in, acc_in, m_ref, acc_ref, rows, heads)

    @pl.when(jnp.logical_not(jnp.logical_or(a_live, b_live)))
    def _():
        m_ref[...] = m_in[...]
        acc_ref[...] = acc_in[...]


def last_kernel(flag_ref, q2_ref, kv_ref, m_in, acc_in, step_ref, w_hbm, out_ref, att_ref, acc_ref, m_ref,
                k2_ref, v2_ref, w_ref, w_sem, *, rows, heads, n_tp):
    w_copy = pltpu.make_async_copy(w_hbm, w_ref, w_sem)
    w_copy.start()

    @pl.when(flag_ref[OTHER + 3] == 1)
    def _():
        spread([kv_ref], k2_ref, v2_ref, 0, rows)
        attend(q2_ref, k2_ref, v2_ref, 4 * rows, m_in, acc_in, m_ref, acc_ref, rows, heads)

    @pl.when(flag_ref[OTHER + 3] == 0)
    def _():
        acc_ref[...] = acc_in[...]

    for h in range(heads):
        cols = slice(h * HEAD, (h + 1) * HEAD)
        acc = acc_ref[h * rows:(h + 1) * rows, :]
        att_ref[:rows, cols] = (acc[:, :HEAD] / acc[:, HEAD:]).astype(jnp.bfloat16)
        att_ref[rows:, cols] = jnp.broadcast_to(step_ref[h:h + 1, :], (STEP_ROWS, HEAD)).astype(jnp.bfloat16)
    w_copy.wait()
    each, wide = rows // n_tp, w_ref.shape[1] // n_tp
    for g in range(n_tp):
        part = jnp.dot(att_ref[...], w_ref[:, g * wide:(g + 1) * wide], preferred_element_type=jnp.float32)
        part = part.astype(jnp.bfloat16)
        for t in range(n_tp):
            out_ref[t, g * each:(g + 1) * each, :] = part[t * each:(t + 1) * each, :]
        out_ref[g, rows:, :] = part[rows:, :]


def sum_kernel(parts_ref, out_ref, step_ref, *, n_tp):
    each, wide = out_ref.shape[0], parts_ref.shape[2]
    rows = parts_ref.shape[1] - STEP_ROWS
    for g in range(n_tp):
        total = parts_ref[0, g * each:(g + 1) * each, :].astype(jnp.float32)
        for t in range(1, n_tp):
            total = total + parts_ref[t, g * each:(g + 1) * each, :].astype(jnp.float32)
        out_ref[:, g * wide:(g + 1) * wide] = total.astype(jnp.bfloat16)
    total = parts_ref[0, rows:, :].astype(jnp.float32)
    for t in range(1, n_tp):
        total = total + parts_ref[t, rows:, :].astype(jnp.float32)
    step_ref[...] = total[:1, :].astype(jnp.bfloat16)


def decode_kernel(len_ref, q_ref, nk_ref, nv_ref, k_hbm, v_hbm, out_ref, k_ref, v_ref, k_sem, v_sem, *, heads):
    k_copy = pltpu.make_async_copy(k_hbm.at[0], k_ref, k_sem)
    v_copy = pltpu.make_async_copy(v_hbm.at[0], v_ref, v_sem)
    k_copy.start()
    v_copy.start()
    query = jnp.concatenate([q_ref[:, h * HEAD:(h + 1) * HEAD] for h in range(heads)], axis=0).astype(jnp.float32)
    scaled = query * SCALE
    high = scaled.astype(jnp.bfloat16)
    low = (scaled - high.astype(jnp.float32)).astype(jnp.bfloat16)
    both = jnp.concatenate([high, low], axis=0)
    own = jnp.sum(query * nk_ref[...].astype(jnp.float32), axis=1, keepdims=True) * SCALE
    k_copy.wait()
    s = lax.dot_general(both, k_ref[...], NT, preferred_element_type=jnp.float32)
    s = s[:heads, :] + s[heads:, :]
    slot = lax.broadcasted_iota(jnp.int32, s.shape, 1)
    s = jnp.where(slot < len_ref[0], s, LOW)
    peak = jnp.maximum(jnp.max(s, axis=1, keepdims=True), own)
    p = jnp.exp2(s - peak)
    own = jnp.exp2(own - peak)
    total = jnp.sum(p, axis=1, keepdims=True) + own
    v_copy.wait()
    mixed = jnp.dot(p.astype(jnp.bfloat16), v_ref[...], preferred_element_type=jnp.float32)
    mixed = mixed + own.astype(jnp.bfloat16).astype(jnp.float32) * nv_ref[...].astype(jnp.float32)
    out_ref[...] = mixed / total


def pack_own_kernel(k_hbm, v_hbm, out_ref, k_sem, v_sem):
    rows = k_hbm.shape[0]
    k_copy = pltpu.make_async_copy(k_hbm, out_ref.at[pl.ds(0, rows)], k_sem)
    v_copy = pltpu.make_async_copy(v_hbm, out_ref.at[pl.ds(rows, rows)], v_sem)
    k_copy.start()
    v_copy.start()
    k_copy.wait()
    v_copy.wait()


def pack_here_kernel(own_ref, y_ref, core_ref, both_ref, far_ref, _, __, here_ref, far_out_ref):
    at = 0
    for ref in (own_ref, y_ref, core_ref, both_ref):
        here_ref[at:at + ref.shape[0], :] = ref[...]
        at += ref.shape[0]
    far_out_ref[...] = far_ref[...]


def gate_kernel(*_):
    pass


def after(block, *others):
    anywhere = pl.BlockSpec(memory_space=pl.ANY)
    return pl.pallas_call(
        gate_kernel,
        in_specs=[anywhere] * (1 + len(others)),
        out_specs=anywhere,
        out_shape=jax.ShapeDtypeStruct(block.shape, block.dtype),
        input_output_aliases={0: 0},
        compiler_params=pltpu.CompilerParams(vmem_limit_bytes=2**20),
        name="gate",
    )(block, *others)


def body(queries, keys, values, out_weight, step_queries, new_keys, new_values, key_cache, value_cache, cache_lens):
    rows = queries.shape[0]
    heads = queries.shape[1] // HEAD
    n_tp = lax.axis_size("tp")
    width = out_weight.shape[1]
    seq = lax.axis_index("seq")
    z, yh, core = seq // (YH * CORE), seq // CORE % YH, seq % CORE
    vmem = pl.BlockSpec(memory_space=pltpu.VMEM)
    smem = pl.BlockSpec(memory_space=pltpu.SMEM)
    anywhere = pl.BlockSpec(memory_space=pl.ANY)

    def params(mib):
        return pltpu.CompilerParams(vmem_limit_bytes=mib * 2**20)

    def cost(keys_seen, more_flops=0):
        return pl.CostEstimate(
            flops=4 * heads * rows * keys_seen * 256 + more_flops,
            bytes_accessed=2**20,
            transcendentals=heads * rows * keys_seen,
        )

    def send(block, pairs):
        return lax.ppermute(block, "seq", pairs)

    own_ring = [jnp.where(core == 0, z >= k, z + k >= Z) for k in range(1, 4)]
    other_ring = [jnp.where(core == 0, z + k >= Z, z >= k) for k in range(1, 4)]
    edges = [jnp.int32(0)] + [jnp.where(c == 1, -rows, rows) for c in (yh, core, yh)]
    flags = jnp.stack([x.astype(jnp.int32) for x in edges + [z >= Z // 2] + own_ring + other_ring])

    own = pl.pallas_call(
        pack_own_kernel,
        in_specs=[anywhere] * 2,
        out_specs=vmem,
        out_shape=jax.ShapeDtypeStruct((2 * rows, HEAD), jnp.bfloat16),
        scratch_shapes=[pltpu.SemaphoreType.DMA] * 2,
        compiler_params=params(60),
        name="pack_own",
    )(keys, values)
    far, by_core, by_y, by_both = (send(own, p) for p in (FAR, SWAP_CORE, SWAP_Y, SWAP_BOTH))
    step_attention = pl.pallas_call(
        functools.partial(decode_kernel, heads=heads),
        in_specs=[smem] + [vmem] * 3 + [anywhere] * 2,
        out_specs=vmem,
        out_shape=jax.ShapeDtypeStruct((heads, HEAD), jnp.float32),
        scratch_shapes=[pltpu.VMEM(key_cache.shape[1:], jnp.bfloat16)] * 2 + [pltpu.SemaphoreType.DMA] * 2,
        compiler_params=params(60),
        cost_estimate=pl.CostEstimate(flops=10**9, bytes_accessed=2 * 2**20, transcendentals=heads * key_cache.shape[1]),
        name="decode",
    )(cache_lens, step_queries, new_keys, new_values, key_cache, value_cache)
    here, far = pl.pallas_call(
        pack_here_kernel,
        in_specs=[vmem] * 5 + [anywhere, smem],
        out_specs=[vmem] * 2,
        out_shape=[jax.ShapeDtypeStruct((n * rows, HEAD), jnp.bfloat16) for n in (8, 2)],
        compiler_params=params(58),
        name="pack_here",
    )(own, by_y, by_core, by_both, far, step_attention, flags)
    ring_1 = send(here, RING)
    fars = [far] + [send(far, p) for p in (SWAP_Y, SWAP_BOTH, SWAP_CORE)]

    state = (
        jax.ShapeDtypeStruct((heads * rows, HEAD), jnp.float32),
        jax.ShapeDtypeStruct((heads * rows, 2 * HEAD), jnp.float32),
    )
    q2, m, acc = pl.pallas_call(
        functools.partial(local_kernel, rows=rows, heads=heads),
        in_specs=[smem, vmem, vmem],
        out_specs=[vmem] * 3,
        out_shape=(jax.ShapeDtypeStruct((heads * rows, 2 * HEAD), jnp.bfloat16),) + state,
        scratch_shapes=[pltpu.VMEM((4 * rows, 2 * HEAD), jnp.bfloat16)] * 2,
        compiler_params=params(36),
        cost_estimate=cost(4 * rows),
        name="attend_local",
    )(flags, queries, here)

    def step(name, at, a, b, m, acc):
        return pl.pallas_call(
            functools.partial(step_kernel, rows=rows, heads=heads, counts=(len(a), len(b)), at=at),
            in_specs=[smem] + [vmem] * (3 + len(a) + len(b)),
            out_specs=[vmem] * 2,
            out_shape=state,
            input_output_aliases={2 + len(a) + len(b): 0, 3 + len(a) + len(b): 1},
            scratch_shapes=[pltpu.VMEM((8 * rows, 2 * HEAD), jnp.bfloat16)] * 2,
            compiler_params=params(36),
            cost_estimate=cost(8 * rows),
            name=name,
        )(flags, q2, *a, *b, m, acc)

    ring_1 = after(ring_1, m)
    ring_2, other_1 = send(ring_1, RING), send(ring_1, SWAP_CORE)
    m, acc = step("attend_1", (OWN + 1, AFAR), [ring_1], fars, m, acc)
    ring_2 = after(ring_2, m)
    ring_3, other_2 = send(ring_2, RING), send(ring_2, SWAP_CORE)
    m, acc = step("attend_2", (OTHER + 1, OWN + 2), [other_1], [ring_2], m, acc)
    ring_3 = after(ring_3, m)
    other_3 = send(ring_3, SWAP_CORE)
    m, acc = step("attend_3", (OTHER + 2, OWN + 3), [other_2], [ring_3], m, acc)

    partial = pl.pallas_call(
        functools.partial(last_kernel, rows=rows, heads=heads, n_tp=n_tp),
        in_specs=[smem] + [vmem] * 5 + [anywhere],
        out_specs=vmem,
        out_shape=jax.ShapeDtypeStruct((n_tp, rows + STEP_ROWS, width // n_tp), jnp.bfloat16),
        scratch_shapes=[
            pltpu.VMEM((rows + STEP_ROWS, heads * HEAD), jnp.bfloat16),
            pltpu.VMEM(state[1].shape, jnp.float32),
            pltpu.VMEM(state[0].shape, jnp.float32),
            pltpu.VMEM((4 * rows, 2 * HEAD), jnp.bfloat16),
            pltpu.VMEM((4 * rows, 2 * HEAD), jnp.bfloat16),
            pltpu.VMEM(out_weight.shape, jnp.bfloat16),
            pltpu.SemaphoreType.DMA,
        ],
        compiler_params=params(44),
        cost_estimate=cost(4 * rows, 2 * rows * heads * HEAD * width),
        name="attend_project",
    )(flags, q2, other_3, m, acc, step_attention, out_weight)
    swapped = lax.all_to_all(partial, "tp", 0, 0)
    prefill_out, decode_out = pl.pallas_call(
        functools.partial(sum_kernel, n_tp=n_tp),
        in_specs=[vmem],
        out_specs=[vmem] * 2,
        out_shape=(
            jax.ShapeDtypeStruct((rows // n_tp, width), jnp.bfloat16),
            jax.ShapeDtypeStruct((1, width // n_tp), jnp.bfloat16),
        ),
        compiler_params=params(24),
        name="sum_parts",
    )(swapped)
    return prefill_out, decode_out


def solution(mesh):
    return jax.shard_map(
        body,
        mesh=mesh,
        in_specs=(
            P("seq", "tp"),
            P("seq", "tp"),
            P("seq", "tp"),
            P("tp", None),
            P("seq", "tp"),
            P("seq", "tp"),
            P("seq", "tp"),
            P("seq", None, "tp"),
            P("seq", None, "tp"),
            P("seq"),
        ),
        out_specs=(P(("seq", "tp"), None), P("seq", "tp")),
        check_vma=False,
    )
```

```python
import functools
import math

import jax
import jax.numpy as jnp
from jax import lax
from jax.experimental import pallas as pl
from jax.experimental.pallas import tpu as pltpu
from jax.sharding import PartitionSpec as P

HEAD = 128
SCALE = HEAD ** -0.5 * math.log2(math.e)
LOW = -1e30
STEP_ROWS = 16
STEP_ROWS = 16
NT = (((1,), (1,)), ((), ()))
EDGES, HALF, OWN, OTHER = 0, 4, 4, 7
Z, YH, CORE = 8, 2, 2


def seq_pairs(move):
    pairs = []
    for z in range(Z):
        for yh in range(YH):
            for c in range(CORE):
                z2, yh2, c2 = move(z, yh, c)
                pairs.append(((z * YH + yh) * CORE + c, ((z2 % Z) * YH + yh2) * CORE + c2))
    return pairs


SWAP_Y = seq_pairs(lambda z, yh, c: (z, 1 - yh, c))
SWAP_CORE = seq_pairs(lambda z, yh, c: (z, yh, 1 - c))
SWAP_BOTH = seq_pairs(lambda z, yh, c: (z, 1 - yh, 1 - c))
FAR = seq_pairs(lambda z, yh, c: (z + Z // 2, yh, c))
RING = seq_pairs(lambda z, yh, c: (z + 1 if c == 0 else z - 1, yh, c))


def split_queries(q_ref, q2_ref, rows, heads):
    for h in range(heads):
        scaled = q_ref[:, h * HEAD:(h + 1) * HEAD].astype(jnp.float32) * SCALE
        high = scaled.astype(jnp.bfloat16)
        low = (scaled - high.astype(jnp.float32)).astype(jnp.bfloat16)
        q2_ref[h * rows:(h + 1) * rows, :HEAD] = high
        q2_ref[h * rows:(h + 1) * rows, HEAD:] = low


def spread(sources, k2_ref, v2_ref, at, rows):
    for src in sources:
        for b in range(src.shape[0] // (2 * rows)):
            k = src[2 * b * rows:(2 * b + 1) * rows, :]
            v = src[(2 * b + 1) * rows:(2 * b + 2) * rows, :]
            k2_ref[at:at + rows, :HEAD] = k
            k2_ref[at:at + rows, HEAD:] = k
            v2_ref[at:at + rows, :HEAD] = v
            v2_ref[at:at + rows, HEAD:] = jnp.ones_like(v)
            at += rows


def attend(q2_ref, k2_ref, v2_ref, n, m_ref, acc_ref, m_out, acc_out, rows, heads, mask=None):
    first = m_ref is None
    together = heads // 2 if heads % 2 == 0 else heads

    def some_heads(i, _):
        parts = [pl.ds(pl.multiple_of((i * together + j) * rows, rows), rows) for j in range(together)]
        scores = [
            lax.dot_general(q2_ref[part, :], k2_ref[:n, :], NT, preferred_element_type=jnp.float32) for part in parts
        ]
        for part, s in zip(parts, scores):
            if mask is not None:
                s = jnp.where(mask, s, LOW)
            peak = jnp.max(s, axis=1, keepdims=True)
            if not first:
                old = m_ref[part, :1]
                peak = jnp.maximum(old, peak)
            p = jnp.exp2(s - peak).astype(jnp.bfloat16)
            mixed = jnp.dot(p, v2_ref[:n, :], preferred_element_type=jnp.float32)
            if not first:
                mixed = mixed + acc_ref[part, :] * jnp.exp2(old - peak)
            acc_out[part, :] = mixed
            m_out[part, :] = jnp.broadcast_to(peak, (rows, HEAD))
        return 0

    lax.fori_loop(0, heads // together, some_heads, 0)


def local_kernel(flag_ref, q_ref, kv_ref, q2_ref, m_ref, acc_ref, k2_ref, v2_ref, *, rows, heads):
    split_queries(q_ref, q2_ref, rows, heads)
    spread([kv_ref], k2_ref, v2_ref, 0, rows)
    row = lax.broadcasted_iota(jnp.int32, (rows, rows), 0)
    col = lax.broadcasted_iota(jnp.int32, (rows, rows), 1)
    mask = jnp.concatenate([(row - col) >= flag_ref[EDGES + b] for b in range(4)], axis=1)
    attend(q2_ref, k2_ref, v2_ref, 4 * rows, None, None, m_ref, acc_ref, rows, heads, mask)


def attend_live(flag_ref, at, q2_ref, groups, k2_ref, v2_ref, m_in, acc_in, m_ref, acc_ref, rows, heads):
    n = 4 * rows
    live = [flag_ref[i] == 1 for i in at]
    if len(groups) == 1:
        some, one = live[0], live[0]
    else:
        some, one = jnp.logical_or(*live), jnp.logical_xor(*live)

        @pl.when(jnp.logical_and(*live))
        def _():
            spread(groups[0], k2_ref, v2_ref, 0, rows)
            spread(groups[1], k2_ref, v2_ref, n, rows)
            attend(q2_ref, k2_ref, v2_ref, 2 * n, m_in, acc_in, m_ref, acc_ref, rows, heads)

    @pl.when(one)
    def _():
        for here, group in zip(live, groups):
            @pl.when(here)
            def _():
                spread(group, k2_ref, v2_ref, 0, rows)

        attend(q2_ref, k2_ref, v2_ref, n, m_in, acc_in, m_ref, acc_ref, rows, heads)

    @pl.when(jnp.logical_not(some))
    def _():
        m_ref[...] = m_in[...]
        acc_ref[...] = acc_in[...]


def step_kernel(flag_ref, q2_ref, *refs, rows, heads, at, counts):
    groups = [refs[:counts[0]], refs[counts[0]:sum(counts)]]
    m_in, acc_in, m_ref, acc_ref, k2_ref, v2_ref = refs[sum(counts):]
    attend_live(flag_ref, at, q2_ref, groups, k2_ref, v2_ref, m_in, acc_in, m_ref, acc_ref, rows, heads)


def last_kernel(flag_ref, q2_ref, other_ref, m_in, acc_in, step_ref, w_hbm, out_ref, att_ref,
                acc_ref, m_ref, k2_ref, v2_ref, w_ref, w_sem, *, rows, heads, n_tp):
    w_copy = pltpu.make_async_copy(w_hbm, w_ref, w_sem)
    w_copy.start()
    attend_live(flag_ref, (OTHER + 3,), q2_ref, [[other_ref]], k2_ref, v2_ref,
                m_in, acc_in, m_ref, acc_ref, rows, heads)
    for h in range(heads):
        cols = slice(h * HEAD, (h + 1) * HEAD)
        acc = acc_ref[h * rows:(h + 1) * rows, :]
        att_ref[:rows, cols] = (acc[:, :HEAD] / acc[:, HEAD:]).astype(jnp.bfloat16)
        att_ref[rows:, cols] = jnp.broadcast_to(step_ref[h:h + 1, :], (STEP_ROWS, HEAD)).astype(jnp.bfloat16)
    w_copy.wait()
    each, wide = rows // n_tp, w_ref.shape[1] // n_tp
    for g in range(n_tp):
        part = jnp.dot(att_ref[...], w_ref[:, g * wide:(g + 1) * wide], preferred_element_type=jnp.float32)
        part = part.astype(jnp.bfloat16)
        for t in range(n_tp):
            out_ref[t, g * each:(g + 1) * each, :] = part[t * each:(t + 1) * each, :]
        out_ref[g, rows:, :] = part[rows:, :]


def sum_kernel(parts_ref, out_ref, step_ref, *, n_tp):
    each, wide = out_ref.shape[0], parts_ref.shape[2]
    rows = parts_ref.shape[1] - STEP_ROWS
    for g in range(n_tp):
        total = parts_ref[0, g * each:(g + 1) * each, :].astype(jnp.float32)
        for t in range(1, n_tp):
            total = total + parts_ref[t, g * each:(g + 1) * each, :].astype(jnp.float32)
        out_ref[:, g * wide:(g + 1) * wide] = total.astype(jnp.bfloat16)
    total = parts_ref[0, rows:, :].astype(jnp.float32)
    for t in range(1, n_tp):
        total = total + parts_ref[t, rows:, :].astype(jnp.float32)
    step_ref[...] = total[:1, :].astype(jnp.bfloat16)


def decode_kernel(len_ref, q_ref, nk_ref, nv_ref, k_hbm, v_hbm, out_ref, k_ref, v_ref, k_sem, v_sem, *, heads):
    k_copy = pltpu.make_async_copy(k_hbm.at[0], k_ref, k_sem)
    v_copy = pltpu.make_async_copy(v_hbm.at[0], v_ref, v_sem)
    k_copy.start()
    v_copy.start()
    query = jnp.concatenate([q_ref[:, h * HEAD:(h + 1) * HEAD] for h in range(heads)], axis=0).astype(jnp.float32)
    scaled = query * SCALE
    high = scaled.astype(jnp.bfloat16)
    low = (scaled - high.astype(jnp.float32)).astype(jnp.bfloat16)
    both = jnp.concatenate([high, low], axis=0)
    own = jnp.sum(query * nk_ref[...].astype(jnp.float32), axis=1, keepdims=True) * SCALE
    k_copy.wait()
    s = lax.dot_general(both, k_ref[...], NT, preferred_element_type=jnp.float32)
    s = s[:heads, :] + s[heads:, :]
    slot = lax.broadcasted_iota(jnp.int32, s.shape, 1)
    s = jnp.where(slot < len_ref[0], s, LOW)
    peak = jnp.maximum(jnp.max(s, axis=1, keepdims=True), own)
    p = jnp.exp2(s - peak)
    own = jnp.exp2(own - peak)
    total = jnp.sum(p, axis=1, keepdims=True) + own
    v_copy.wait()
    mixed = jnp.dot(p.astype(jnp.bfloat16), v_ref[...], preferred_element_type=jnp.float32)
    mixed = mixed + own.astype(jnp.bfloat16).astype(jnp.float32) * nv_ref[...].astype(jnp.float32)
    out_ref[...] = mixed / total


def pack_own_kernel(k_hbm, v_hbm, out_ref, k_sem, v_sem):
    rows = k_hbm.shape[0]
    k_copy = pltpu.make_async_copy(k_hbm, out_ref.at[pl.ds(0, rows)], k_sem)
    v_copy = pltpu.make_async_copy(v_hbm, out_ref.at[pl.ds(rows, rows)], v_sem)
    k_copy.start()
    v_copy.start()
    k_copy.wait()
    v_copy.wait()


def pack_here_kernel(own_ref, both_ref, core_ref, far_ref, y_ref, _, here_ref, far_out_ref):
    at = 0
    for ref in (own_ref, y_ref, core_ref, both_ref):
        here_ref[at:at + ref.shape[0], :] = ref[...]
        at += ref.shape[0]
    far_out_ref[...] = far_ref[...]


def gate_kernel(*_):
    pass


def after(block, *others):
    anywhere = pl.BlockSpec(memory_space=pl.ANY)
    return pl.pallas_call(
        gate_kernel,
        in_specs=[anywhere] * (1 + len(others)),
        out_specs=anywhere,
        out_shape=jax.ShapeDtypeStruct(block.shape, block.dtype),
        input_output_aliases={0: 0},
        compiler_params=pltpu.CompilerParams(vmem_limit_bytes=2**20),
        name="gate",
    )(block, *others)


def body(queries, keys, values, out_weight, step_queries, new_keys, new_values, key_cache, value_cache, cache_lens):
    rows = queries.shape[0]
    heads = queries.shape[1] // HEAD
    n_tp = lax.axis_size("tp")
    width = out_weight.shape[1]
    seq = lax.axis_index("seq")
    z, yh, core = seq // (YH * CORE), seq // CORE % YH, seq % CORE
    vmem = pl.BlockSpec(memory_space=pltpu.VMEM)
    smem = pl.BlockSpec(memory_space=pltpu.SMEM)
    anywhere = pl.BlockSpec(memory_space=pl.ANY)

    def params(mib):
        return pltpu.CompilerParams(vmem_limit_bytes=mib * 2**20)

    def cost(keys_seen, more_flops=0):
        return pl.CostEstimate(
            flops=4 * heads * rows * keys_seen * 256 + more_flops,
            bytes_accessed=2**20,
            transcendentals=heads * rows * keys_seen,
        )

    def send(block, pairs):
        return lax.ppermute(block, "seq", pairs)

    own_ring = [jnp.where(core == 0, z >= k, z + k >= Z) for k in range(1, 4)]
    other_ring = [jnp.where(core == 0, z + k >= Z, z >= k) for k in range(1, 4)]
    edges = [jnp.int32(0)] + [jnp.where(c == 1, -rows, rows) for c in (yh, core, yh)]
    flags = jnp.stack([x.astype(jnp.int32) for x in edges + [z >= Z // 2] + own_ring + other_ring])

    own = pl.pallas_call(
        pack_own_kernel,
        in_specs=[anywhere] * 2,
        out_specs=vmem,
        out_shape=jax.ShapeDtypeStruct((2 * rows, HEAD), jnp.bfloat16),
        scratch_shapes=[pltpu.SemaphoreType.DMA] * 2,
        compiler_params=params(60),
        name="pack_own",
    )(keys, values)
    by_core, far, by_y = (send(own, p) for p in (SWAP_CORE, FAR, SWAP_Y))
    step_attention = pl.pallas_call(
        functools.partial(decode_kernel, heads=heads),
        in_specs=[smem] + [vmem] * 3 + [anywhere] * 2,
        out_specs=vmem,
        out_shape=jax.ShapeDtypeStruct((heads, HEAD), jnp.float32),
        scratch_shapes=[pltpu.VMEM(key_cache.shape[1:], jnp.bfloat16)] * 2 + [pltpu.SemaphoreType.DMA] * 2,
        compiler_params=params(60),
        cost_estimate=pl.CostEstimate(flops=10**9, bytes_accessed=2 * 2**20, transcendentals=heads * key_cache.shape[1]),
        name="decode",
    )(cache_lens, step_queries, new_keys, new_values, key_cache, value_cache)
    by_y = after(by_y, step_attention)
    by_both = send(by_y, SWAP_CORE)
    here, far = pl.pallas_call(
        pack_here_kernel,
        in_specs=[vmem] * 5 + [smem],
        out_specs=[vmem] * 2,
        out_shape=[jax.ShapeDtypeStruct((n * rows, HEAD), jnp.bfloat16) for n in (8, 2)],
        compiler_params=params(4),
        name="pack_here",
    )(own, by_both, by_core, far, by_y, flags)
    ring_1 = send(here, RING)
    fars = [far] + [send(far, p) for p in (SWAP_CORE, SWAP_BOTH, SWAP_Y)]

    state = (
        jax.ShapeDtypeStruct((heads * rows, HEAD), jnp.float32),
        jax.ShapeDtypeStruct((heads * rows, 2 * HEAD), jnp.float32),
    )
    q2, m, acc = pl.pallas_call(
        functools.partial(local_kernel, rows=rows, heads=heads),
        in_specs=[smem, vmem, vmem],
        out_specs=[vmem] * 3,
        out_shape=(jax.ShapeDtypeStruct((heads * rows, 2 * HEAD), jnp.bfloat16),) + state,
        scratch_shapes=[pltpu.VMEM((4 * rows, 2 * HEAD), jnp.bfloat16)] * 2,
        compiler_params=params(36),
        cost_estimate=cost(4 * rows),
        name="attend_local",
    )(flags, queries, here)

    def step(name, at, groups, m, acc):
        counts = [len(group) for group in groups]
        n = sum(counts)
        return pl.pallas_call(
            functools.partial(step_kernel, rows=rows, heads=heads, at=at, counts=counts),
            in_specs=[smem] + [vmem] * (3 + n),
            out_specs=[vmem] * 2,
            out_shape=state,
            input_output_aliases={2 + n: 0, 3 + n: 1},
            scratch_shapes=[pltpu.VMEM((8 * rows, 2 * HEAD), jnp.bfloat16)] * 2,
            compiler_params=params(36),
            cost_estimate=cost(8 * rows),
            name=name,
        )(flags, q2, *groups[0], *groups[1], m, acc)

    ring_1 = after(ring_1, m)
    ring_2, other_1 = send(ring_1, RING), send(ring_1, SWAP_CORE)
    m, acc = step("attend_1", (OWN + 1, HALF), [[ring_1], fars], m, acc)
    ring_2 = after(ring_2, m)
    ring_3, other_2 = send(ring_2, RING), send(ring_2, SWAP_CORE)
    m, acc = step("attend_2", (OTHER + 1, OWN + 2), [[other_1], [ring_2]], m, acc)
    ring_3 = after(ring_3, m)
    other_3 = send(ring_3, SWAP_CORE)
    m, acc = step("attend_3", (OTHER + 2, OWN + 3), [[other_2], [ring_3]], m, acc)

    partial = pl.pallas_call(
        functools.partial(last_kernel, rows=rows, heads=heads, n_tp=n_tp),
        in_specs=[smem] + [vmem] * 5 + [anywhere],
        out_specs=vmem,
        out_shape=jax.ShapeDtypeStruct((n_tp, rows + STEP_ROWS, width // n_tp), jnp.bfloat16),
        scratch_shapes=[
            pltpu.VMEM((rows + STEP_ROWS, heads * HEAD), jnp.bfloat16),
            pltpu.VMEM(state[1].shape, jnp.float32),
            pltpu.VMEM(state[0].shape, jnp.float32),
            pltpu.VMEM((4 * rows, 2 * HEAD), jnp.bfloat16),
            pltpu.VMEM((4 * rows, 2 * HEAD), jnp.bfloat16),
            pltpu.VMEM(out_weight.shape, jnp.bfloat16),
            pltpu.SemaphoreType.DMA,
        ],
        compiler_params=params(44),
        cost_estimate=cost(4 * rows, 2 * rows * heads * HEAD * width),
        name="attend_project",
    )(flags, q2, other_3, m, acc, step_attention, out_weight)
    swapped = lax.all_to_all(partial, "tp", 0, 0)
    prefill_out, decode_out = pl.pallas_call(
        functools.partial(sum_kernel, n_tp=n_tp),
        in_specs=[vmem],
        out_specs=[vmem] * 2,
        out_shape=(
            jax.ShapeDtypeStruct((rows // n_tp, width), jnp.bfloat16),
            jax.ShapeDtypeStruct((1, width // n_tp), jnp.bfloat16),
        ),
        compiler_params=params(24),
        name="sum_parts",
    )(swapped)
    return prefill_out, decode_out


def solution(mesh):
    return jax.shard_map(
        body,
        mesh=mesh,
        in_specs=(
            P("seq", "tp"),
            P("seq", "tp"),
            P("seq", "tp"),
            P("tp", None),
            P("seq", "tp"),
            P("seq", "tp"),
            P("seq", "tp"),
            P("seq", None, "tp"),
            P("seq", None, "tp"),
            P("seq"),
        ),
        out_specs=(P(("seq", "tp"), None), P("seq", "tp")),
        check_vma=False,
    )
```

```python
import functools
import math

import jax
import jax.numpy as jnp
from jax import lax
from jax.experimental import pallas as pl
from jax.experimental.pallas import tpu as pltpu
from jax.sharding import PartitionSpec as P

HEAD = 128
SCALE = HEAD ** -0.5 * math.log2(math.e)
LOW = -1e30
LANES = 128
STEP_ROWS = 16
LANES = 128
STEP_ROWS = 16
NT = (((1,), (1,)), ((), ()))
EDGES, HALF, OWN, OTHER, START = 0, 4, 4, 7, 11
Z, YH, CORE = 8, 2, 2


def seq_pairs(move):
    pairs = []
    for z in range(Z):
        for yh in range(YH):
            for c in range(CORE):
                z2, yh2, c2 = move(z, yh, c)
                pairs.append(((z * YH + yh) * CORE + c, ((z2 % Z) * YH + yh2) * CORE + c2))
    return pairs


SWAP_Y = seq_pairs(lambda z, yh, c: (z, 1 - yh, c))
SWAP_CORE = seq_pairs(lambda z, yh, c: (z, yh, 1 - c))
SWAP_BOTH = seq_pairs(lambda z, yh, c: (z, 1 - yh, 1 - c))
FAR = seq_pairs(lambda z, yh, c: (z + Z // 2, yh, c))
RING = seq_pairs(lambda z, yh, c: (z + 1 if c == 0 else z - 1, yh, c))


X, YL = 4, 2
OVER_Y = [(x * YL + y, x * YL + 1 - y) for x in range(X) for y in range(YL)]


def over_x_pairs(dx):
    return [(x * YL + y, (x + dx) % X * YL + y) for x in range(X) for y in range(YL)]


def split_queries(flag_ref, q_ref, q2_ref, rows, heads, n_tp):
    each = rows // n_tp
    for i in range(n_tp):
        start = pl.multiple_of(flag_ref[START + i], each)
        for h in range(heads):
            scaled = q_ref[pl.ds(start, each), h * HEAD:(h + 1) * HEAD].astype(jnp.float32) * SCALE
            high = scaled.astype(jnp.bfloat16)
            low = (scaled - high.astype(jnp.float32)).astype(jnp.bfloat16)
            at = h * rows + i * each
            q2_ref[at:at + each, :HEAD] = high
            q2_ref[at:at + each, HEAD:] = low


def spread(sources, k2_ref, v2_ref, at, rows):
    for src in sources:
        for b in range(src.shape[0] // (2 * rows)):
            k = src[2 * b * rows:(2 * b + 1) * rows, :]
            v = src[(2 * b + 1) * rows:(2 * b + 2) * rows, :]
            k2_ref[at:at + rows, :HEAD] = k
            k2_ref[at:at + rows, HEAD:] = k
            v2_ref[at:at + rows, :HEAD] = v
            v2_ref[at:at + rows, HEAD:] = jnp.ones_like(v)
            at += rows


def attend(q2_ref, k2_ref, v2_ref, n, m_ref, acc_ref, m_out, acc_out, rows, heads, mask=None):
    first = m_ref is None
    together = heads // 2 if heads % 2 == 0 else heads

    def some_heads(i, _):
        parts = [pl.ds(pl.multiple_of((i * together + j) * rows, rows), rows) for j in range(together)]
        scores = [
            lax.dot_general(q2_ref[part, :], k2_ref[:n, :], NT, preferred_element_type=jnp.float32) for part in parts
        ]
        for part, s in zip(parts, scores):
            if mask is not None:
                s = jnp.where(mask, s, LOW)
            peak = jnp.max(s, axis=1, keepdims=True)
            if not first:
                old = m_ref[part, :1]
                peak = jnp.maximum(old, peak)
            p = jnp.exp2(s - peak).astype(jnp.bfloat16)
            mixed = jnp.dot(p, v2_ref[:n, :], preferred_element_type=jnp.float32)
            if not first:
                mixed = mixed + acc_ref[part, :] * jnp.exp2(old - peak)
            acc_out[part, :] = mixed
            m_out[part, :] = jnp.broadcast_to(peak, (rows, HEAD))
        return 0

    lax.fori_loop(0, heads // together, some_heads, 0)


def local_kernel(flag_ref, q_ref, kv_ref, q2_ref, m_ref, acc_ref, k2_ref, v2_ref, *, rows, heads, n_tp):
    split_queries(flag_ref, q_ref, q2_ref, rows, heads, n_tp)
    spread([kv_ref], k2_ref, v2_ref, 0, rows)
    each = rows // n_tp
    place = lax.broadcasted_iota(jnp.int32, (rows, rows), 0)
    row = place
    for i in range(n_tp):
        inside = jnp.logical_and(place >= i * each, place < (i + 1) * each)
        row = jnp.where(inside, place + (flag_ref[START + i] - i * each), row)
    col = lax.broadcasted_iota(jnp.int32, (rows, rows), 1)
    mask = jnp.concatenate([(row - col) >= flag_ref[EDGES + b] for b in range(4)], axis=1)
    attend(q2_ref, k2_ref, v2_ref, 4 * rows, None, None, m_ref, acc_ref, rows, heads, mask)


def attend_live(flag_ref, at, q2_ref, groups, k2_ref, v2_ref, m_in, acc_in, m_ref, acc_ref, rows, heads):
    n = 4 * rows
    live = [flag_ref[i] == 1 for i in at]
    if len(groups) == 1:
        some, one = live[0], live[0]
    else:
        some, one = jnp.logical_or(*live), jnp.logical_xor(*live)

        @pl.when(jnp.logical_and(*live))
        def _():
            spread(groups[0], k2_ref, v2_ref, 0, rows)
            spread(groups[1], k2_ref, v2_ref, n, rows)
            attend(q2_ref, k2_ref, v2_ref, 2 * n, m_in, acc_in, m_ref, acc_ref, rows, heads)

    @pl.when(one)
    def _():
        for here, group in zip(live, groups):
            @pl.when(here)
            def _():
                spread(group, k2_ref, v2_ref, 0, rows)

        attend(q2_ref, k2_ref, v2_ref, n, m_in, acc_in, m_ref, acc_ref, rows, heads)

    @pl.when(jnp.logical_not(some))
    def _():
        m_ref[...] = m_in[...]
        acc_ref[...] = acc_in[...]


def step_kernel(flag_ref, q2_ref, *refs, rows, heads, at, counts):
    groups = [refs[:counts[0]], refs[counts[0]:sum(counts)]]
    m_in, acc_in, m_ref, acc_ref, k2_ref, v2_ref = refs[sum(counts):]
    attend_live(flag_ref, at, q2_ref, groups, k2_ref, v2_ref, m_in, acc_in, m_ref, acc_ref, rows, heads)


def last_kernel(flag_ref, q2_ref, other_ref, m_in, acc_in, step_ref, w_hbm, keep_ref, send_ref, g0_ref, g1_ref, g2_ref,
                g3_ref, att_ref, acc_ref, m_ref, k2_ref, v2_ref, w_ref, token_ref, w_sem, *, rows, heads, n_tp):
    w_copy = pltpu.make_async_copy(w_hbm, w_ref, w_sem)
    w_copy.start()
    attend_live(flag_ref, (OTHER + 3,), q2_ref, [[other_ref]], k2_ref, v2_ref,
                m_in, acc_in, m_ref, acc_ref, rows, heads)
    for h in range(heads):
        cols = slice(h * HEAD, (h + 1) * HEAD)
        acc = acc_ref[h * rows:(h + 1) * rows, :]
        att_ref[:rows, cols] = (acc[:, :HEAD] / acc[:, HEAD:]).astype(jnp.bfloat16)
        att_ref[rows:, cols] = jnp.broadcast_to(step_ref[h:h + 1, :], (STEP_ROWS, HEAD)).astype(jnp.bfloat16)
    w_copy.wait()
    each, wide, half = rows // n_tp, w_ref.shape[1] // n_tp, w_ref.shape[1] // 2
    g_refs = (g0_ref, g1_ref, g2_ref, g3_ref)
    for g in range(n_tp):
        part = jnp.dot(att_ref[...], w_ref[:, g * wide:(g + 1) * wide], preferred_element_type=jnp.float32)
        token_ref[:, g * wide:(g + 1) * wide] = part[rows:, :]
        part = part.astype(jnp.bfloat16)
        if g * wide < half:
            cols = slice(g * wide, (g + 1) * wide)
            keep_ref[:, cols] = part[:rows // 2, :]
            send_ref[:, cols] = part[rows // 2:rows, :]
        else:
            cols = slice(g * wide - half, (g + 1) * wide - half)
            for dx, g_ref in enumerate(g_refs):
                g_ref[:each, cols] = part[dx * each:(dx + 1) * each, :]
                g_ref[each:2 * each, cols] = part[rows // 2 + dx * each:rows // 2 + (dx + 1) * each, :]
    for g_ref in g_refs:
        g_ref[:, half:] = jnp.zeros((2 * each, LANES), jnp.bfloat16)
    for i in range(n_tp):
        dy, dx = divmod(i, X)
        start = pl.multiple_of(flag_ref[START + i] * (wide // each), wide)
        for j in range(wide // LANES):
            piece = token_ref[:1, pl.ds(start + j * LANES, LANES)].astype(jnp.bfloat16)
            g_refs[dx][dy * each + j:dy * each + j + 1, half:] = piece


def middle_kernel(keep_ref, recv_ref, g0_ref, g1_ref, g2_ref, g3_ref, f0_ref, f1_ref, f2_ref, f3_ref, mine_ref, give_ref):
    each = f0_ref.shape[0]
    for dx, f_ref in enumerate((f0_ref, f1_ref, f2_ref, f3_ref)):
        part = slice(dx * each, (dx + 1) * each)
        total = keep_ref[part, :].astype(jnp.float32) + recv_ref[part, :].astype(jnp.float32)
        f_ref[...] = total.astype(f_ref.dtype)
    for at, ref in ((0, mine_ref), (each, give_ref)):
        total = g0_ref[at:at + each, :].astype(jnp.float32)
        for g_ref in (g1_ref, g2_ref, g3_ref):
            total = total + g_ref[at:at + each, :].astype(jnp.float32)
        ref[...] = total.astype(ref.dtype)


def sum_kernel(f0_ref, f1_ref, f2_ref, f3_ref, mine_ref, give_ref, out_ref, step_ref):
    half = f0_ref.shape[1]
    total = f0_ref[...]
    for ref in (f1_ref, f2_ref, f3_ref):
        total = total + ref[...].astype(jnp.float32)
    out_ref[:, :half] = total.astype(jnp.bfloat16)
    total = mine_ref[...] + give_ref[...].astype(jnp.float32)
    out_ref[:, half:] = total[:, :half].astype(jnp.bfloat16)
    for j in range(step_ref.shape[1] // LANES):
        step_ref[:, j * LANES:(j + 1) * LANES] = total[j:j + 1, half:].astype(jnp.bfloat16)


def decode_kernel(len_ref, q_ref, nk_ref, nv_ref, k_hbm, v_hbm, out_ref, k_ref, v_ref, k_sem, v_sem, *, heads):
    k_copy = pltpu.make_async_copy(k_hbm.at[0], k_ref, k_sem)
    v_copy = pltpu.make_async_copy(v_hbm.at[0], v_ref, v_sem)
    k_copy.start()
    v_copy.start()
    query = jnp.concatenate([q_ref[:, h * HEAD:(h + 1) * HEAD] for h in range(heads)], axis=0).astype(jnp.float32)
    scaled = query * SCALE
    high = scaled.astype(jnp.bfloat16)
    low = (scaled - high.astype(jnp.float32)).astype(jnp.bfloat16)
    both = jnp.concatenate([high, low], axis=0)
    own = jnp.sum(query * nk_ref[...].astype(jnp.float32), axis=1, keepdims=True) * SCALE
    k_copy.wait()
    s = lax.dot_general(both, k_ref[...], NT, preferred_element_type=jnp.float32)
    s = s[:heads, :] + s[heads:, :]
    slot = lax.broadcasted_iota(jnp.int32, s.shape, 1)
    s = jnp.where(slot < len_ref[0], s, LOW)
    peak = jnp.maximum(jnp.max(s, axis=1, keepdims=True), own)
    p = jnp.exp2(s - peak)
    own = jnp.exp2(own - peak)
    total = jnp.sum(p, axis=1, keepdims=True) + own
    v_copy.wait()
    mixed = jnp.dot(p.astype(jnp.bfloat16), v_ref[...], preferred_element_type=jnp.float32)
    mixed = mixed + own.astype(jnp.bfloat16).astype(jnp.float32) * nv_ref[...].astype(jnp.float32)
    out_ref[...] = mixed / total


def pack_own_kernel(k_hbm, v_hbm, out_ref, k_sem, v_sem):
    rows = k_hbm.shape[0]
    k_copy = pltpu.make_async_copy(k_hbm, out_ref.at[pl.ds(0, rows)], k_sem)
    v_copy = pltpu.make_async_copy(v_hbm, out_ref.at[pl.ds(rows, rows)], v_sem)
    k_copy.start()
    v_copy.start()
    k_copy.wait()
    v_copy.wait()


def pack_here_kernel(own_ref, both_ref, core_ref, far_ref, y_ref, _, here_ref, far_out_ref):
    at = 0
    for ref in (own_ref, y_ref, core_ref, both_ref):
        here_ref[at:at + ref.shape[0], :] = ref[...]
        at += ref.shape[0]
    far_out_ref[...] = far_ref[...]


def gate_kernel(*_):
    pass


def after(block, *others):
    anywhere = pl.BlockSpec(memory_space=pl.ANY)
    return pl.pallas_call(
        gate_kernel,
        in_specs=[anywhere] * (1 + len(others)),
        out_specs=anywhere,
        out_shape=jax.ShapeDtypeStruct(block.shape, block.dtype),
        input_output_aliases={0: 0},
        compiler_params=pltpu.CompilerParams(vmem_limit_bytes=2**20),
        name="gate",
    )(block, *others)


def body(queries, keys, values, out_weight, step_queries, new_keys, new_values, key_cache, value_cache, cache_lens):
    rows = queries.shape[0]
    heads = queries.shape[1] // HEAD
    n_tp = lax.axis_size("tp")
    width = out_weight.shape[1]
    seq = lax.axis_index("seq")
    z, yh, core = seq // (YH * CORE), seq // CORE % YH, seq % CORE
    vmem = pl.BlockSpec(memory_space=pltpu.VMEM)
    smem = pl.BlockSpec(memory_space=pltpu.SMEM)
    anywhere = pl.BlockSpec(memory_space=pl.ANY)

    def params(mib):
        return pltpu.CompilerParams(vmem_limit_bytes=mib * 2**20)

    def cost(keys_seen, more_flops=0):
        return pl.CostEstimate(
            flops=4 * heads * rows * keys_seen * 256 + more_flops,
            bytes_accessed=2**20,
            transcendentals=heads * rows * keys_seen,
        )

    def send(block, pairs):
        return lax.ppermute(block, "seq", pairs)

    own_ring = [jnp.where(core == 0, z >= k, z + k >= Z) for k in range(1, 4)]
    other_ring = [jnp.where(core == 0, z + k >= Z, z >= k) for k in range(1, 4)]
    edges = [jnp.int32(0)] + [jnp.where(c == 1, -rows, rows) for c in (yh, core, yh)]
    tp = lax.axis_index("tp")
    starts = [
        ((tp // YL + dx) % X * YL + (tp % YL + dy) % YL) * (rows // n_tp) for dy in range(YL) for dx in range(X)
    ]
    flags = jnp.stack([x.astype(jnp.int32) for x in edges + [z >= Z // 2] + own_ring + other_ring + starts])

    own = pl.pallas_call(
        pack_own_kernel,
        in_specs=[anywhere] * 2,
        out_specs=vmem,
        out_shape=jax.ShapeDtypeStruct((2 * rows, HEAD), jnp.bfloat16),
        scratch_shapes=[pltpu.SemaphoreType.DMA] * 2,
        compiler_params=params(60),
        name="pack_own",
    )(keys, values)
    by_core, far, by_y = (send(own, p) for p in (SWAP_CORE, FAR, SWAP_Y))
    step_attention = pl.pallas_call(
        functools.partial(decode_kernel, heads=heads),
        in_specs=[smem] + [vmem] * 3 + [anywhere] * 2,
        out_specs=vmem,
        out_shape=jax.ShapeDtypeStruct((heads, HEAD), jnp.float32),
        scratch_shapes=[pltpu.VMEM(key_cache.shape[1:], jnp.bfloat16)] * 2 + [pltpu.SemaphoreType.DMA] * 2,
        compiler_params=params(60),
        cost_estimate=pl.CostEstimate(flops=10**9, bytes_accessed=2 * 2**20, transcendentals=heads * key_cache.shape[1]),
        name="decode",
    )(cache_lens, step_queries, new_keys, new_values, key_cache, value_cache)
    by_y = after(by_y, step_attention)
    by_both = send(by_y, SWAP_CORE)
    here, far = pl.pallas_call(
        pack_here_kernel,
        in_specs=[vmem] * 5 + [smem],
        out_specs=[vmem] * 2,
        out_shape=[jax.ShapeDtypeStruct((n * rows, HEAD), jnp.bfloat16) for n in (8, 2)],
        compiler_params=params(4),
        name="pack_here",
    )(own, by_both, by_core, far, by_y, flags)
    ring_1 = send(here, RING)
    fars = [far] + [send(far, p) for p in (SWAP_CORE, SWAP_BOTH, SWAP_Y)]

    state = (
        jax.ShapeDtypeStruct((heads * rows, HEAD), jnp.float32),
        jax.ShapeDtypeStruct((heads * rows, 2 * HEAD), jnp.float32),
    )
    q2, m, acc = pl.pallas_call(
        functools.partial(local_kernel, rows=rows, heads=heads, n_tp=n_tp),
        in_specs=[smem, vmem, vmem],
        out_specs=[vmem] * 3,
        out_shape=(jax.ShapeDtypeStruct((heads * rows, 2 * HEAD), jnp.bfloat16),) + state,
        scratch_shapes=[pltpu.VMEM((4 * rows, 2 * HEAD), jnp.bfloat16)] * 2,
        compiler_params=params(36),
        cost_estimate=cost(4 * rows),
        name="attend_local",
    )(flags, queries, here)

    def step(name, at, groups, m, acc):
        counts = [len(group) for group in groups]
        n = sum(counts)
        return pl.pallas_call(
            functools.partial(step_kernel, rows=rows, heads=heads, at=at, counts=counts),
            in_specs=[smem] + [vmem] * (3 + n),
            out_specs=[vmem] * 2,
            out_shape=state,
            input_output_aliases={2 + n: 0, 3 + n: 1},
            scratch_shapes=[pltpu.VMEM((8 * rows, 2 * HEAD), jnp.bfloat16)] * 2,
            compiler_params=params(36),
            cost_estimate=cost(8 * rows),
            name=name,
        )(flags, q2, *groups[0], *groups[1], m, acc)

    ring_1 = after(ring_1, m)
    ring_2, other_1 = send(ring_1, RING), send(ring_1, SWAP_CORE)
    m, acc = step("attend_1", (OWN + 1, HALF), [[ring_1], fars], m, acc)
    ring_2 = after(ring_2, m)
    ring_3, other_2 = send(ring_2, RING), send(ring_2, SWAP_CORE)
    m, acc = step("attend_2", (OTHER + 1, OWN + 2), [[other_1], [ring_2]], m, acc)
    ring_3 = after(ring_3, m)
    other_3 = send(ring_3, SWAP_CORE)
    m, acc = step("attend_3", (OTHER + 2, OWN + 3), [[other_2], [ring_3]], m, acc)

    each, half = rows // n_tp, width // 2
    bf16 = functools.partial(jax.ShapeDtypeStruct, dtype=jnp.bfloat16)
    keep, give_y, *over_x = pl.pallas_call(
        functools.partial(last_kernel, rows=rows, heads=heads, n_tp=n_tp),
        in_specs=[smem] + [vmem] * 5 + [anywhere],
        out_specs=[vmem] * 6,
        out_shape=[bf16((rows // 2, half))] * 2 + [bf16((2 * each, half + LANES))] * X,
        scratch_shapes=[
            pltpu.VMEM((rows + STEP_ROWS, heads * HEAD), jnp.bfloat16),
            pltpu.VMEM(state[1].shape, jnp.float32),
            pltpu.VMEM(state[0].shape, jnp.float32),
            pltpu.VMEM((4 * rows, 2 * HEAD), jnp.bfloat16),
            pltpu.VMEM((4 * rows, 2 * HEAD), jnp.bfloat16),
            pltpu.VMEM(out_weight.shape, jnp.bfloat16),
            pltpu.VMEM((STEP_ROWS, width), jnp.float32),
            pltpu.SemaphoreType.DMA,
        ],
        compiler_params=params(44),
        cost_estimate=cost(4 * rows, 2 * rows * heads * HEAD * width),
        name="attend_project",
    )(flags, q2, other_3, m, acc, step_attention, out_weight)
    from_y = lax.ppermute(give_y, "tp", OVER_Y)
    from_x = [lax.ppermute(over_x[dx], "tp", over_x_pairs(dx)) for dx in (1, 2, 3)]
    f0, *give_x, mine, give = pl.pallas_call(
        middle_kernel,
        in_specs=[vmem] * 6,
        out_specs=[vmem] * 6,
        out_shape=[jax.ShapeDtypeStruct((each, half), jnp.float32)] + [bf16((each, half))] * 3
        + [jax.ShapeDtypeStruct((each, half + LANES), jnp.float32), bf16((each, half + LANES))],
        compiler_params=params(24),
        name="sum_first",
    )(keep, from_y, over_x[0], *from_x)
    given = lax.ppermute(give, "tp", OVER_Y)
    given_x = [lax.ppermute(give_x[dx - 1], "tp", over_x_pairs(dx)) for dx in (1, 2, 3)]
    prefill_out, decode_out = pl.pallas_call(
        sum_kernel,
        in_specs=[vmem] * 6,
        out_specs=[vmem] * 2,
        out_shape=[bf16((each, width)), bf16((1, width // n_tp))],
        compiler_params=params(24),
        name="sum_last",
    )(f0, *given_x, mine, given)
    return prefill_out, decode_out


def solution(mesh):
    return jax.shard_map(
        body,
        mesh=mesh,
        in_specs=(
            P("seq", "tp"),
            P("seq", "tp"),
            P("seq", "tp"),
            P("tp", None),
            P("seq", "tp"),
            P("seq", "tp"),
            P("seq", "tp"),
            P("seq", None, "tp"),
            P("seq", None, "tp"),
            P("seq"),
        ),
        out_specs=(P(("seq", "tp"), None), P("seq", "tp")),
        check_vma=False,
    )
```

```python
import functools
import math

import jax
import jax.numpy as jnp
from jax import lax
from jax.experimental import pallas as pl
from jax.experimental.pallas import tpu as pltpu
from jax.sharding import PartitionSpec as P

HEAD = 128
SCALE = HEAD ** -0.5 * math.log2(math.e)
LOW = -1e30
LANES = 128
STEP_ROWS = 16
LANES = 128
STEP_ROWS = 16
NT = (((1,), (1,)), ((), ()))
EDGES, HALF, OWN, OTHER, START = 0, 4, 4, 7, 11
Z, YH, CORE = 8, 2, 2


def seq_pairs(move):
    pairs = []
    for z in range(Z):
        for yh in range(YH):
            for c in range(CORE):
                z2, yh2, c2 = move(z, yh, c)
                pairs.append(((z * YH + yh) * CORE + c, ((z2 % Z) * YH + yh2) * CORE + c2))
    return pairs


SWAP_Y = seq_pairs(lambda z, yh, c: (z, 1 - yh, c))
SWAP_CORE = seq_pairs(lambda z, yh, c: (z, yh, 1 - c))
SWAP_BOTH = seq_pairs(lambda z, yh, c: (z, 1 - yh, 1 - c))
FAR = seq_pairs(lambda z, yh, c: (z + Z // 2, yh, c))
RING = seq_pairs(lambda z, yh, c: (z + 1 if c == 0 else z - 1, yh, c))


X, YL = 4, 2
OVER_Y = [(x * YL + y, x * YL + 1 - y) for x in range(X) for y in range(YL)]


def over_x_pairs(dx):
    return [(x * YL + y, (x + dx) % X * YL + y) for x in range(X) for y in range(YL)]


def split_queries(flag_ref, q_ref, q2_ref, rows, heads, n_tp):
    each = rows // n_tp
    for i in range(n_tp):
        start = pl.multiple_of(flag_ref[START + i], each)
        for h in range(heads):
            scaled = q_ref[pl.ds(start, each), h * HEAD:(h + 1) * HEAD].astype(jnp.float32) * SCALE
            high = scaled.astype(jnp.bfloat16)
            low = (scaled - high.astype(jnp.float32)).astype(jnp.bfloat16)
            at = h * rows + i * each
            q2_ref[at:at + each, :HEAD] = high
            q2_ref[at:at + each, HEAD:] = low


def spread(sources, k2_ref, v2_ref, at, rows):
    for src in sources:
        for b in range(src.shape[0] // (2 * rows)):
            k = src[2 * b * rows:(2 * b + 1) * rows, :]
            v = src[(2 * b + 1) * rows:(2 * b + 2) * rows, :]
            k2_ref[at:at + rows, :HEAD] = k
            k2_ref[at:at + rows, HEAD:] = k
            v2_ref[at:at + rows, :HEAD] = v
            v2_ref[at:at + rows, HEAD:] = jnp.ones_like(v)
            at += rows


def attend(q2_ref, k2_ref, v2_ref, n, m_ref, acc_ref, m_out, acc_out, rows, heads, mask=None):
    first = m_ref is None
    together = heads // 2 if heads % 2 == 0 else heads

    def some_heads(i, _):
        parts = [pl.ds(pl.multiple_of((i * together + j) * rows, rows), rows) for j in range(together)]
        scores = [
            lax.dot_general(q2_ref[part, :], k2_ref[:n, :], NT, preferred_element_type=jnp.float32) for part in parts
        ]
        for part, s in zip(parts, scores):
            if mask is not None:
                s = jnp.where(mask, s, LOW)
            peak = jnp.max(s, axis=1, keepdims=True)
            if not first:
                old = m_ref[part, :1]
                peak = jnp.maximum(old, peak)
            p = jnp.exp2(s - peak).astype(jnp.bfloat16)
            mixed = jnp.dot(p, v2_ref[:n, :], preferred_element_type=jnp.float32)
            if not first:
                mixed = mixed + acc_ref[part, :] * jnp.exp2(old - peak)
            acc_out[part, :] = mixed
            m_out[part, :] = jnp.broadcast_to(peak, (rows, HEAD))
        return 0

    lax.fori_loop(0, heads // together, some_heads, 0)


def local_kernel(flag_ref, q_ref, kv_ref, q2_ref, m_ref, acc_ref, k2_ref, v2_ref, *, rows, heads, n_tp):
    split_queries(flag_ref, q_ref, q2_ref, rows, heads, n_tp)
    spread([kv_ref], k2_ref, v2_ref, 0, rows)
    each = rows // n_tp
    place = lax.broadcasted_iota(jnp.int32, (rows, rows), 0)
    row = place
    for i in range(n_tp):
        inside = jnp.logical_and(place >= i * each, place < (i + 1) * each)
        row = jnp.where(inside, place + (flag_ref[START + i] - i * each), row)
    col = lax.broadcasted_iota(jnp.int32, (rows, rows), 1)
    mask = jnp.concatenate([(row - col) >= flag_ref[EDGES + b] for b in range(4)], axis=1)
    attend(q2_ref, k2_ref, v2_ref, 4 * rows, None, None, m_ref, acc_ref, rows, heads, mask)


def attend_live(flag_ref, at, q2_ref, groups, k2_ref, v2_ref, m_in, acc_in, m_ref, acc_ref, rows, heads):
    n = 4 * rows
    live = [flag_ref[i] == 1 for i in at]
    if len(groups) == 1:
        some, one = live[0], live[0]
    else:
        some, one = jnp.logical_or(*live), jnp.logical_xor(*live)

        @pl.when(jnp.logical_and(*live))
        def _():
            spread(groups[0], k2_ref, v2_ref, 0, rows)
            spread(groups[1], k2_ref, v2_ref, n, rows)
            attend(q2_ref, k2_ref, v2_ref, 2 * n, m_in, acc_in, m_ref, acc_ref, rows, heads)

    @pl.when(one)
    def _():
        for here, group in zip(live, groups):
            @pl.when(here)
            def _():
                spread(group, k2_ref, v2_ref, 0, rows)

        attend(q2_ref, k2_ref, v2_ref, n, m_in, acc_in, m_ref, acc_ref, rows, heads)

    @pl.when(jnp.logical_not(some))
    def _():
        m_ref[...] = m_in[...]
        acc_ref[...] = acc_in[...]


def step_kernel(flag_ref, q2_ref, *refs, rows, heads, at, counts):
    groups = [refs[:counts[0]], refs[counts[0]:sum(counts)]]
    m_in, acc_in, m_ref, acc_ref, k2_ref, v2_ref = refs[sum(counts):]
    attend_live(flag_ref, at, q2_ref, groups, k2_ref, v2_ref, m_in, acc_in, m_ref, acc_ref, rows, heads)


def last_kernel(flag_ref, q2_ref, other_ref, m_in, acc_in, step_ref, w_hbm, keep_ref, send_ref, g0_ref, g1_ref, g2_ref,
                g3_ref, att_ref, acc_ref, m_ref, k2_ref, v2_ref, w_ref, token_ref, w_sem, *, rows, heads, n_tp):
    w_copy = pltpu.make_async_copy(w_hbm, w_ref, w_sem)
    w_copy.start()
    attend_live(flag_ref, (OTHER + 3,), q2_ref, [[other_ref]], k2_ref, v2_ref,
                m_in, acc_in, m_ref, acc_ref, rows, heads)
    for h in range(heads):
        cols = slice(h * HEAD, (h + 1) * HEAD)
        acc = acc_ref[h * rows:(h + 1) * rows, :]
        att_ref[:rows, cols] = (acc[:, :HEAD] / acc[:, HEAD:]).astype(jnp.bfloat16)
        att_ref[rows:, cols] = jnp.broadcast_to(step_ref[h:h + 1, :], (STEP_ROWS, HEAD)).astype(jnp.bfloat16)
    w_copy.wait()
    each, wide, split, piece = rows // n_tp, w_ref.shape[1] // n_tp, keep_ref.shape[1], 256
    g_refs = (g0_ref, g1_ref, g2_ref, g3_ref)
    for c in range(0, w_ref.shape[1], piece):
        part = jnp.dot(att_ref[...], w_ref[:, c:c + piece], preferred_element_type=jnp.float32)
        token_ref[:, c:c + piece] = part[rows:, :]
        part = part.astype(jnp.bfloat16)
        if c < split:
            keep_ref[:, c:c + piece] = part[:rows // 2, :]
            send_ref[:, c:c + piece] = part[rows // 2:rows, :]
        else:
            cols = slice(c - split, c - split + piece)
            for dx, g_ref in enumerate(g_refs):
                g_ref[:each, cols] = part[dx * each:(dx + 1) * each, :]
                g_ref[each:2 * each, cols] = part[rows // 2 + dx * each:rows // 2 + (dx + 1) * each, :]
    for g_ref in g_refs:
        g_ref[:, -LANES:] = jnp.zeros((2 * each, LANES), jnp.bfloat16)
    for i in range(n_tp):
        dy, dx = divmod(i, X)
        start = pl.multiple_of(flag_ref[START + i] * (wide // each), wide)
        for j in range(wide // LANES):
            chunk = token_ref[:1, pl.ds(start + j * LANES, LANES)].astype(jnp.bfloat16)
            g_refs[dx][dy * each + j:dy * each + j + 1, -LANES:] = chunk


def middle_kernel(keep_ref, recv_ref, g0_ref, g1_ref, g2_ref, g3_ref, f0_ref, f1_ref, f2_ref, f3_ref, mine_ref, give_ref):
    each = f0_ref.shape[0]
    for dx, f_ref in enumerate((f0_ref, f1_ref, f2_ref, f3_ref)):
        part = slice(dx * each, (dx + 1) * each)
        total = keep_ref[part, :].astype(jnp.float32) + recv_ref[part, :].astype(jnp.float32)
        f_ref[...] = total.astype(f_ref.dtype)
    for at, ref in ((0, mine_ref), (each, give_ref)):
        total = g0_ref[at:at + each, :].astype(jnp.float32)
        for g_ref in (g1_ref, g2_ref, g3_ref):
            total = total + g_ref[at:at + each, :].astype(jnp.float32)
        ref[...] = total.astype(ref.dtype)


def sum_kernel(f0_ref, f1_ref, f2_ref, f3_ref, mine_ref, give_ref, out_ref, step_ref):
    split, rest = f0_ref.shape[1], mine_ref.shape[1] - LANES
    total = f0_ref[...]
    for ref in (f1_ref, f2_ref, f3_ref):
        total = total + ref[...].astype(jnp.float32)
    out_ref[:, :split] = total.astype(jnp.bfloat16)
    total = mine_ref[...] + give_ref[...].astype(jnp.float32)
    out_ref[:, split:] = total[:, :rest].astype(jnp.bfloat16)
    for j in range(step_ref.shape[1] // LANES):
        step_ref[:, j * LANES:(j + 1) * LANES] = total[j:j + 1, rest:].astype(jnp.bfloat16)


def decode_kernel(len_ref, q_ref, nk_ref, nv_ref, k_hbm, v_hbm, out_ref, k_ref, v_ref, k_sem, v_sem, *, heads):
    k_copy = pltpu.make_async_copy(k_hbm.at[0], k_ref, k_sem)
    v_copy = pltpu.make_async_copy(v_hbm.at[0], v_ref, v_sem)
    k_copy.start()
    v_copy.start()
    query = jnp.concatenate([q_ref[:, h * HEAD:(h + 1) * HEAD] for h in range(heads)], axis=0).astype(jnp.float32)
    scaled = query * SCALE
    high = scaled.astype(jnp.bfloat16)
    low = (scaled - high.astype(jnp.float32)).astype(jnp.bfloat16)
    both = jnp.concatenate([high, low], axis=0)
    own = jnp.sum(query * nk_ref[...].astype(jnp.float32), axis=1, keepdims=True) * SCALE
    k_copy.wait()
    s = lax.dot_general(both, k_ref[...], NT, preferred_element_type=jnp.float32)
    s = s[:heads, :] + s[heads:, :]
    slot = lax.broadcasted_iota(jnp.int32, s.shape, 1)
    s = jnp.where(slot < len_ref[0], s, LOW)
    peak = jnp.maximum(jnp.max(s, axis=1, keepdims=True), own)
    p = jnp.exp2(s - peak)
    own = jnp.exp2(own - peak)
    total = jnp.sum(p, axis=1, keepdims=True) + own
    v_copy.wait()
    mixed = jnp.dot(p.astype(jnp.bfloat16), v_ref[...], preferred_element_type=jnp.float32)
    mixed = mixed + own.astype(jnp.bfloat16).astype(jnp.float32) * nv_ref[...].astype(jnp.float32)
    out_ref[...] = mixed / total


def pack_own_kernel(k_hbm, v_hbm, out_ref, k_sem, v_sem):
    rows = k_hbm.shape[0]
    k_copy = pltpu.make_async_copy(k_hbm, out_ref.at[pl.ds(0, rows)], k_sem)
    v_copy = pltpu.make_async_copy(v_hbm, out_ref.at[pl.ds(rows, rows)], v_sem)
    k_copy.start()
    v_copy.start()
    k_copy.wait()
    v_copy.wait()


def pack_here_kernel(own_ref, both_ref, core_ref, far_ref, y_ref, _, here_ref, far_out_ref):
    at = 0
    for ref in (own_ref, y_ref, core_ref, both_ref):
        here_ref[at:at + ref.shape[0], :] = ref[...]
        at += ref.shape[0]
    far_out_ref[...] = far_ref[...]


def gate_kernel(*_):
    pass


def after(block, *others):
    anywhere = pl.BlockSpec(memory_space=pl.ANY)
    return pl.pallas_call(
        gate_kernel,
        in_specs=[anywhere] * (1 + len(others)),
        out_specs=anywhere,
        out_shape=jax.ShapeDtypeStruct(block.shape, block.dtype),
        input_output_aliases={0: 0},
        compiler_params=pltpu.CompilerParams(vmem_limit_bytes=2**20),
        name="gate",
    )(block, *others)


def body(queries, keys, values, out_weight, step_queries, new_keys, new_values, key_cache, value_cache, cache_lens):
    rows = queries.shape[0]
    heads = queries.shape[1] // HEAD
    n_tp = lax.axis_size("tp")
    width = out_weight.shape[1]
    seq = lax.axis_index("seq")
    z, yh, core = seq // (YH * CORE), seq // CORE % YH, seq % CORE
    vmem = pl.BlockSpec(memory_space=pltpu.VMEM)
    smem = pl.BlockSpec(memory_space=pltpu.SMEM)
    anywhere = pl.BlockSpec(memory_space=pl.ANY)

    def params(mib):
        return pltpu.CompilerParams(vmem_limit_bytes=mib * 2**20)

    def cost(keys_seen, more_flops=0):
        return pl.CostEstimate(
            flops=4 * heads * rows * keys_seen * 256 + more_flops,
            bytes_accessed=2**20,
            transcendentals=heads * rows * keys_seen,
        )

    def send(block, pairs):
        return lax.ppermute(block, "seq", pairs)

    own_ring = [jnp.where(core == 0, z >= k, z + k >= Z) for k in range(1, 4)]
    other_ring = [jnp.where(core == 0, z + k >= Z, z >= k) for k in range(1, 4)]
    edges = [jnp.int32(0)] + [jnp.where(c == 1, -rows, rows) for c in (yh, core, yh)]
    tp = lax.axis_index("tp")
    starts = [
        ((tp // YL + dx) % X * YL + (tp % YL + dy) % YL) * (rows // n_tp) for dy in range(YL) for dx in range(X)
    ]
    flags = jnp.stack([x.astype(jnp.int32) for x in edges + [z >= Z // 2] + own_ring + other_ring + starts])

    own = pl.pallas_call(
        pack_own_kernel,
        in_specs=[anywhere] * 2,
        out_specs=vmem,
        out_shape=jax.ShapeDtypeStruct((2 * rows, HEAD), jnp.bfloat16),
        scratch_shapes=[pltpu.SemaphoreType.DMA] * 2,
        compiler_params=params(60),
        name="pack_own",
    )(keys, values)
    by_core, far, by_y = (send(own, p) for p in (SWAP_CORE, FAR, SWAP_Y))
    step_attention = pl.pallas_call(
        functools.partial(decode_kernel, heads=heads),
        in_specs=[smem] + [vmem] * 3 + [anywhere] * 2,
        out_specs=vmem,
        out_shape=jax.ShapeDtypeStruct((heads, HEAD), jnp.float32),
        scratch_shapes=[pltpu.VMEM(key_cache.shape[1:], jnp.bfloat16)] * 2 + [pltpu.SemaphoreType.DMA] * 2,
        compiler_params=params(60),
        cost_estimate=pl.CostEstimate(flops=10**9, bytes_accessed=2 * 2**20, transcendentals=heads * key_cache.shape[1]),
        name="decode",
    )(cache_lens, step_queries, new_keys, new_values, key_cache, value_cache)
    by_y = after(by_y, step_attention)
    by_both = send(by_y, SWAP_CORE)
    here, far = pl.pallas_call(
        pack_here_kernel,
        in_specs=[vmem] * 5 + [smem],
        out_specs=[vmem] * 2,
        out_shape=[jax.ShapeDtypeStruct((n * rows, HEAD), jnp.bfloat16) for n in (8, 2)],
        compiler_params=params(4),
        name="pack_here",
    )(own, by_both, by_core, far, by_y, flags)
    ring_1 = send(here, RING)
    fars = [far] + [send(far, p) for p in (SWAP_CORE, SWAP_BOTH, SWAP_Y)]

    state = (
        jax.ShapeDtypeStruct((heads * rows, HEAD), jnp.float32),
        jax.ShapeDtypeStruct((heads * rows, 2 * HEAD), jnp.float32),
    )
    q2, m, acc = pl.pallas_call(
        functools.partial(local_kernel, rows=rows, heads=heads, n_tp=n_tp),
        in_specs=[smem, vmem, vmem],
        out_specs=[vmem] * 3,
        out_shape=(jax.ShapeDtypeStruct((heads * rows, 2 * HEAD), jnp.bfloat16),) + state,
        scratch_shapes=[pltpu.VMEM((4 * rows, 2 * HEAD), jnp.bfloat16)] * 2,
        compiler_params=params(36),
        cost_estimate=cost(4 * rows),
        name="attend_local",
    )(flags, queries, here)

    def step(name, at, groups, m, acc):
        counts = [len(group) for group in groups]
        n = sum(counts)
        return pl.pallas_call(
            functools.partial(step_kernel, rows=rows, heads=heads, at=at, counts=counts),
            in_specs=[smem] + [vmem] * (3 + n),
            out_specs=[vmem] * 2,
            out_shape=state,
            input_output_aliases={2 + n: 0, 3 + n: 1},
            scratch_shapes=[pltpu.VMEM((8 * rows, 2 * HEAD), jnp.bfloat16)] * 2,
            compiler_params=params(36),
            cost_estimate=cost(8 * rows),
            name=name,
        )(flags, q2, *groups[0], *groups[1], m, acc)

    ring_1 = after(ring_1, m)
    ring_2, other_1 = send(ring_1, RING), send(ring_1, SWAP_CORE)
    m, acc = step("attend_1", (OWN + 1, HALF), [[ring_1], fars], m, acc)
    ring_2 = after(ring_2, m)
    ring_3, other_2 = send(ring_2, RING), send(ring_2, SWAP_CORE)
    m, acc = step("attend_2", (OTHER + 1, OWN + 2), [[other_1], [ring_2]], m, acc)
    ring_3 = after(ring_3, m)
    other_3 = send(ring_3, SWAP_CORE)
    m, acc = step("attend_3", (OTHER + 2, OWN + 3), [[other_2], [ring_3]], m, acc)

    each, split = rows // n_tp, width * 9 // 16
    bf16 = functools.partial(jax.ShapeDtypeStruct, dtype=jnp.bfloat16)
    keep, give_y, *over_x = pl.pallas_call(
        functools.partial(last_kernel, rows=rows, heads=heads, n_tp=n_tp),
        in_specs=[smem] + [vmem] * 5 + [anywhere],
        out_specs=[vmem] * 6,
        out_shape=[bf16((rows // 2, split))] * 2 + [bf16((2 * each, width - split + LANES))] * X,
        scratch_shapes=[
            pltpu.VMEM((rows + STEP_ROWS, heads * HEAD), jnp.bfloat16),
            pltpu.VMEM(state[1].shape, jnp.float32),
            pltpu.VMEM(state[0].shape, jnp.float32),
            pltpu.VMEM((4 * rows, 2 * HEAD), jnp.bfloat16),
            pltpu.VMEM((4 * rows, 2 * HEAD), jnp.bfloat16),
            pltpu.VMEM(out_weight.shape, jnp.bfloat16),
            pltpu.VMEM((STEP_ROWS, width), jnp.float32),
            pltpu.SemaphoreType.DMA,
        ],
        compiler_params=params(44),
        cost_estimate=cost(4 * rows, 2 * rows * heads * HEAD * width),
        name="attend_project",
    )(flags, q2, other_3, m, acc, step_attention, out_weight)
    from_y = lax.ppermute(give_y, "tp", OVER_Y)
    from_x = [lax.ppermute(over_x[dx], "tp", over_x_pairs(dx)) for dx in (1, 2, 3)]
    f0, *give_x, mine, give = pl.pallas_call(
        middle_kernel,
        in_specs=[vmem] * 6,
        out_specs=[vmem] * 6,
        out_shape=[jax.ShapeDtypeStruct((each, split), jnp.float32)] + [bf16((each, split))] * 3
        + [jax.ShapeDtypeStruct((each, width - split + LANES), jnp.float32), bf16((each, width - split + LANES))],
        compiler_params=params(24),
        name="sum_first",
    )(keep, from_y, over_x[0], *from_x)
    given = lax.ppermute(give, "tp", OVER_Y)
    given_x = [lax.ppermute(give_x[dx - 1], "tp", over_x_pairs(dx)) for dx in (1, 2, 3)]
    prefill_out, decode_out = pl.pallas_call(
        sum_kernel,
        in_specs=[vmem] * 6,
        out_specs=[vmem] * 2,
        out_shape=[bf16((each, width)), bf16((1, width // n_tp))],
        compiler_params=params(24),
        name="sum_last",
    )(f0, *given_x, mine, given)
    return prefill_out, decode_out


def solution(mesh):
    return jax.shard_map(
        body,
        mesh=mesh,
        in_specs=(
            P("seq", "tp"),
            P("seq", "tp"),
            P("seq", "tp"),
            P("tp", None),
            P("seq", "tp"),
            P("seq", "tp"),
            P("seq", "tp"),
            P("seq", None, "tp"),
            P("seq", None, "tp"),
            P("seq"),
        ),
        out_specs=(P(("seq", "tp"), None), P("seq", "tp")),
        check_vma=False,
    )
```

```python
import functools
import math

import jax
import jax.numpy as jnp
from jax import lax
from jax.experimental import pallas as pl
from jax.experimental.pallas import tpu as pltpu
from jax.sharding import PartitionSpec as P

HEAD = 128
SCALE = HEAD ** -0.5 * math.log2(math.e)
LOW = -1e30
LANES = 128
STEP_ROWS = 16
LANES = 128
STEP_ROWS = 16
NT = (((1,), (1,)), ((), ()))
EDGES, HALF, OWN, OTHER, START = 0, 4, 4, 7, 11
Z, YH, CORE = 8, 2, 2


def seq_pairs(move):
    pairs = []
    for z in range(Z):
        for yh in range(YH):
            for c in range(CORE):
                z2, yh2, c2 = move(z, yh, c)
                pairs.append(((z * YH + yh) * CORE + c, ((z2 % Z) * YH + yh2) * CORE + c2))
    return pairs


SWAP_Y = seq_pairs(lambda z, yh, c: (z, 1 - yh, c))
SWAP_CORE = seq_pairs(lambda z, yh, c: (z, yh, 1 - c))
SWAP_BOTH = seq_pairs(lambda z, yh, c: (z, 1 - yh, 1 - c))
FAR = seq_pairs(lambda z, yh, c: (z + Z // 2 if z < Z // 2 else Z - 1 - z, yh, c))
RING = seq_pairs(lambda z, yh, c: (z + 1 if c == 0 else z - 1, yh, c))


X, YL = 4, 2
OVER_Y = [(x * YL + y, x * YL + 1 - y) for x in range(X) for y in range(YL)]


def over_x_pairs(dx):
    return [(x * YL + y, (x + dx) % X * YL + y) for x in range(X) for y in range(YL)]


def split_queries(flag_ref, q_ref, q2_ref, rows, heads, n_tp):
    each = rows // n_tp
    for i in range(n_tp):
        start = pl.multiple_of(flag_ref[START + i], each)
        for h in range(heads):
            scaled = q_ref[pl.ds(start, each), h * HEAD:(h + 1) * HEAD].astype(jnp.float32) * SCALE
            high = scaled.astype(jnp.bfloat16)
            low = (scaled - high.astype(jnp.float32)).astype(jnp.bfloat16)
            at = h * rows + i * each
            q2_ref[at:at + each, :HEAD] = high
            q2_ref[at:at + each, HEAD:] = low


def spread(sources, k2_ref, v2_ref, at, rows):
    for src in sources:
        for b in range(src.shape[0] // (2 * rows)):
            k = src[2 * b * rows:(2 * b + 1) * rows, :]
            v = src[(2 * b + 1) * rows:(2 * b + 2) * rows, :]
            k2_ref[at:at + rows, :HEAD] = k
            k2_ref[at:at + rows, HEAD:] = k
            v2_ref[at:at + rows, :HEAD] = v
            v2_ref[at:at + rows, HEAD:] = jnp.ones_like(v)
            at += rows


def attend(q2_ref, k2_ref, v2_ref, n, m_ref, acc_ref, m_out, acc_out, rows, heads, mask=None):
    first = m_ref is None
    together = heads // 2 if heads % 2 == 0 else heads

    def some_heads(i, _):
        parts = [pl.ds(pl.multiple_of((i * together + j) * rows, rows), rows) for j in range(together)]
        scores = [
            lax.dot_general(q2_ref[part, :], k2_ref[:n, :], NT, preferred_element_type=jnp.float32) for part in parts
        ]
        for part, s in zip(parts, scores):
            if mask is not None:
                s = jnp.where(mask, s, LOW)
            peak = jnp.max(s, axis=1, keepdims=True)
            if not first:
                old = m_ref[part, :1]
                peak = jnp.maximum(old, peak)
            p = jnp.exp2(s - peak).astype(jnp.bfloat16)
            mixed = jnp.dot(p, v2_ref[:n, :], preferred_element_type=jnp.float32)
            if not first:
                mixed = mixed + acc_ref[part, :] * jnp.exp2(old - peak)
            acc_out[part, :] = mixed
            m_out[part, :] = jnp.broadcast_to(peak, (rows, HEAD))
        return 0

    lax.fori_loop(0, heads // together, some_heads, 0)


def local_kernel(flag_ref, q_ref, kv_ref, q2_ref, m_ref, acc_ref, k2_ref, v2_ref, *, rows, heads, n_tp):
    split_queries(flag_ref, q_ref, q2_ref, rows, heads, n_tp)
    spread([kv_ref], k2_ref, v2_ref, 0, rows)
    each = rows // n_tp
    place = lax.broadcasted_iota(jnp.int32, (rows, rows), 0)
    row = place
    for i in range(n_tp):
        inside = jnp.logical_and(place >= i * each, place < (i + 1) * each)
        row = jnp.where(inside, place + (flag_ref[START + i] - i * each), row)
    col = lax.broadcasted_iota(jnp.int32, (rows, rows), 1)
    mask = jnp.concatenate([(row - col) >= flag_ref[EDGES + b] for b in range(4)], axis=1)
    attend(q2_ref, k2_ref, v2_ref, 4 * rows, None, None, m_ref, acc_ref, rows, heads, mask)


def attend_live(flag_ref, at, q2_ref, groups, k2_ref, v2_ref, m_in, acc_in, m_ref, acc_ref, rows, heads):
    n = 4 * rows
    live = [flag_ref[i] == 1 for i in at]
    if len(groups) == 1:
        some, one = live[0], live[0]
    else:
        some, one = jnp.logical_or(*live), jnp.logical_xor(*live)

        @pl.when(jnp.logical_and(*live))
        def _():
            spread(groups[0], k2_ref, v2_ref, 0, rows)
            spread(groups[1], k2_ref, v2_ref, n, rows)
            attend(q2_ref, k2_ref, v2_ref, 2 * n, m_in, acc_in, m_ref, acc_ref, rows, heads)

    @pl.when(one)
    def _():
        for here, group in zip(live, groups):
            @pl.when(here)
            def _():
                spread(group, k2_ref, v2_ref, 0, rows)

        attend(q2_ref, k2_ref, v2_ref, n, m_in, acc_in, m_ref, acc_ref, rows, heads)

    @pl.when(jnp.logical_not(some))
    def _():
        m_ref[...] = m_in[...]
        acc_ref[...] = acc_in[...]


def step_kernel(flag_ref, q2_ref, *refs, rows, heads, at, counts):
    groups = [refs[:counts[0]], refs[counts[0]:sum(counts)]]
    m_in, acc_in, m_ref, acc_ref, k2_ref, v2_ref = refs[sum(counts):]
    attend_live(flag_ref, at, q2_ref, groups, k2_ref, v2_ref, m_in, acc_in, m_ref, acc_ref, rows, heads)


def last_kernel(flag_ref, q2_ref, other_ref, m_in, acc_in, step_ref, w_hbm, keep_ref, send_ref, g0_ref, g1_ref, g2_ref,
                g3_ref, att_ref, acc_ref, m_ref, k2_ref, v2_ref, w_ref, token_ref, w_sem, *, rows, heads, n_tp):
    w_copy = pltpu.make_async_copy(w_hbm, w_ref, w_sem)
    w_copy.start()
    attend_live(flag_ref, (OTHER + 3,), q2_ref, [[other_ref]], k2_ref, v2_ref,
                m_in, acc_in, m_ref, acc_ref, rows, heads)
    for h in range(heads):
        cols = slice(h * HEAD, (h + 1) * HEAD)
        acc = acc_ref[h * rows:(h + 1) * rows, :]
        att_ref[:rows, cols] = (acc[:, :HEAD] / acc[:, HEAD:]).astype(jnp.bfloat16)
        att_ref[rows:, cols] = jnp.broadcast_to(step_ref[h:h + 1, :], (STEP_ROWS, HEAD)).astype(jnp.bfloat16)
    w_copy.wait()
    each, wide, split, piece = rows // n_tp, w_ref.shape[1] // n_tp, keep_ref.shape[1], 256
    g_refs = (g0_ref, g1_ref, g2_ref, g3_ref)
    for c in range(0, w_ref.shape[1], piece):
        part = jnp.dot(att_ref[...], w_ref[:, c:c + piece], preferred_element_type=jnp.float32)
        token_ref[:, c:c + piece] = part[rows:, :]
        part = part.astype(jnp.bfloat16)
        if c < split:
            keep_ref[:, c:c + piece] = part[:rows // 2, :]
            send_ref[:, c:c + piece] = part[rows // 2:rows, :]
        else:
            cols = slice(c - split, c - split + piece)
            for dx, g_ref in enumerate(g_refs):
                g_ref[:each, cols] = part[dx * each:(dx + 1) * each, :]
                g_ref[each:2 * each, cols] = part[rows // 2 + dx * each:rows // 2 + (dx + 1) * each, :]
    line = lax.broadcasted_iota(jnp.int32, (each, LANES), 0)
    for i in range(n_tp):
        dy, dx = divmod(i, X)
        start = pl.multiple_of(flag_ref[START + i] * (wide // each), wide)
        tile = jnp.zeros((each, LANES), jnp.float32)
        for j in range(wide // LANES):
            tile = jnp.where(line == j, token_ref[:1, pl.ds(start + j * LANES, LANES)], tile)
        g_refs[dx][dy * each:(dy + 1) * each, -LANES:] = tile.astype(jnp.bfloat16)


def middle_kernel(keep_ref, recv_ref, g0_ref, g1_ref, g2_ref, g3_ref, f0_ref, f1_ref, f2_ref, f3_ref, mine_ref, give_ref):
    each = f0_ref.shape[0]
    for dx, f_ref in enumerate((f0_ref, f1_ref, f2_ref, f3_ref)):
        part = slice(dx * each, (dx + 1) * each)
        total = keep_ref[part, :].astype(jnp.float32) + recv_ref[part, :].astype(jnp.float32)
        f_ref[...] = total.astype(f_ref.dtype)
    for at, ref in ((0, mine_ref), (each, give_ref)):
        total = g0_ref[at:at + each, :].astype(jnp.float32)
        for g_ref in (g1_ref, g2_ref, g3_ref):
            total = total + g_ref[at:at + each, :].astype(jnp.float32)
        ref[...] = total.astype(ref.dtype)


def sum_kernel(f0_ref, f1_ref, f2_ref, f3_ref, mine_ref, give_ref, out_ref, step_ref):
    split, rest = f0_ref.shape[1], mine_ref.shape[1] - LANES
    total = f0_ref[...]
    for ref in (f1_ref, f2_ref, f3_ref):
        total = total + ref[...].astype(jnp.float32)
    out_ref[:, :split] = total.astype(jnp.bfloat16)
    total = mine_ref[...] + give_ref[...].astype(jnp.float32)
    out_ref[:, split:] = total[:, :rest].astype(jnp.bfloat16)
    for j in range(step_ref.shape[1] // LANES):
        step_ref[:, j * LANES:(j + 1) * LANES] = total[j:j + 1, rest:].astype(jnp.bfloat16)


def decode_kernel(len_ref, q_ref, nk_ref, nv_ref, k_hbm, v_hbm, out_ref, k_ref, v_ref, k_sem, v_sem, *, heads):
    k_copy = pltpu.make_async_copy(k_hbm.at[0], k_ref, k_sem)
    v_copy = pltpu.make_async_copy(v_hbm.at[0], v_ref, v_sem)
    k_copy.start()
    v_copy.start()
    query = jnp.concatenate([q_ref[:, h * HEAD:(h + 1) * HEAD] for h in range(heads)], axis=0).astype(jnp.float32)
    scaled = query * SCALE
    high = scaled.astype(jnp.bfloat16)
    low = (scaled - high.astype(jnp.float32)).astype(jnp.bfloat16)
    both = jnp.concatenate([high, low], axis=0)
    own = jnp.sum(query * nk_ref[...].astype(jnp.float32), axis=1, keepdims=True) * SCALE
    k_copy.wait()
    s = lax.dot_general(both, k_ref[...], NT, preferred_element_type=jnp.float32)
    s = s[:heads, :] + s[heads:, :]
    slot = lax.broadcasted_iota(jnp.int32, s.shape, 1)
    s = jnp.where(slot < len_ref[0], s, LOW)
    peak = jnp.maximum(jnp.max(s, axis=1, keepdims=True), own)
    p = jnp.exp2(s - peak)
    own = jnp.exp2(own - peak)
    total = jnp.sum(p, axis=1, keepdims=True) + own
    v_copy.wait()
    mixed = jnp.dot(p.astype(jnp.bfloat16), v_ref[...], preferred_element_type=jnp.float32)
    mixed = mixed + own.astype(jnp.bfloat16).astype(jnp.float32) * nv_ref[...].astype(jnp.float32)
    out_ref[...] = mixed / total


def pack_own_kernel(k_hbm, v_hbm, out_ref, k_sem, v_sem):
    rows = k_hbm.shape[0]
    k_copy = pltpu.make_async_copy(k_hbm, out_ref.at[pl.ds(0, rows)], k_sem)
    v_copy = pltpu.make_async_copy(v_hbm, out_ref.at[pl.ds(rows, rows)], v_sem)
    k_copy.start()
    v_copy.start()
    k_copy.wait()
    v_copy.wait()


def pack_here_kernel(own_ref, both_ref, core_ref, far_ref, y_ref, _, here_ref, far_out_ref):
    at = 0
    for ref in (own_ref, y_ref, core_ref, both_ref):
        here_ref[at:at + ref.shape[0], :] = ref[...]
        at += ref.shape[0]
    far_out_ref[...] = far_ref[...]


def gate_kernel(*_):
    pass


def after(block, *others):
    anywhere = pl.BlockSpec(memory_space=pl.ANY)
    return pl.pallas_call(
        gate_kernel,
        in_specs=[anywhere] * (1 + len(others)),
        out_specs=anywhere,
        out_shape=jax.ShapeDtypeStruct(block.shape, block.dtype),
        input_output_aliases={0: 0},
        compiler_params=pltpu.CompilerParams(vmem_limit_bytes=2**20),
        name="gate",
    )(block, *others)


def body(queries, keys, values, out_weight, step_queries, new_keys, new_values, key_cache, value_cache, cache_lens):
    rows = queries.shape[0]
    heads = queries.shape[1] // HEAD
    n_tp = lax.axis_size("tp")
    width = out_weight.shape[1]
    seq = lax.axis_index("seq")
    z, yh, core = seq // (YH * CORE), seq // CORE % YH, seq % CORE
    vmem = pl.BlockSpec(memory_space=pltpu.VMEM)
    smem = pl.BlockSpec(memory_space=pltpu.SMEM)
    anywhere = pl.BlockSpec(memory_space=pl.ANY)

    def params(mib):
        return pltpu.CompilerParams(vmem_limit_bytes=mib * 2**20)

    def cost(keys_seen, more_flops=0):
        return pl.CostEstimate(
            flops=4 * heads * rows * keys_seen * 256 + more_flops,
            bytes_accessed=2**20,
            transcendentals=heads * rows * keys_seen,
        )

    def send(block, pairs):
        return lax.ppermute(block, "seq", pairs)

    own_ring = [jnp.where(core == 0, z >= k, z + k >= Z) for k in range(1, 4)]
    other_ring = [jnp.where(core == 0, z + k >= Z, z >= k) for k in range(1, 4)]
    edges = [jnp.int32(0)] + [jnp.where(c == 1, -rows, rows) for c in (yh, core, yh)]
    tp = lax.axis_index("tp")
    starts = [
        ((tp // YL + dx) % X * YL + (tp % YL + dy) % YL) * (rows // n_tp) for dy in range(YL) for dx in range(X)
    ]
    flags = jnp.stack([x.astype(jnp.int32) for x in edges + [z >= Z // 2] + own_ring + other_ring + starts])

    own = pl.pallas_call(
        pack_own_kernel,
        in_specs=[anywhere] * 2,
        out_specs=vmem,
        out_shape=jax.ShapeDtypeStruct((2 * rows, HEAD), jnp.bfloat16),
        scratch_shapes=[pltpu.SemaphoreType.DMA] * 2,
        compiler_params=params(60),
        name="pack_own",
    )(keys, values)
    by_core, far, by_y = (send(own, p) for p in (SWAP_CORE, FAR, SWAP_Y))
    step_attention = pl.pallas_call(
        functools.partial(decode_kernel, heads=heads),
        in_specs=[smem] + [vmem] * 3 + [anywhere] * 2,
        out_specs=vmem,
        out_shape=jax.ShapeDtypeStruct((heads, HEAD), jnp.float32),
        scratch_shapes=[pltpu.VMEM(key_cache.shape[1:], jnp.bfloat16)] * 2 + [pltpu.SemaphoreType.DMA] * 2,
        compiler_params=params(60),
        cost_estimate=pl.CostEstimate(flops=10**9, bytes_accessed=2 * 2**20, transcendentals=heads * key_cache.shape[1]),
        name="decode",
    )(cache_lens, step_queries, new_keys, new_values, key_cache, value_cache)
    by_y = after(by_y, step_attention)
    by_both = send(by_y, SWAP_CORE)
    here, far = pl.pallas_call(
        pack_here_kernel,
        in_specs=[vmem] * 5 + [smem],
        out_specs=[vmem] * 2,
        out_shape=[jax.ShapeDtypeStruct((n * rows, HEAD), jnp.bfloat16) for n in (8, 2)],
        compiler_params=params(4),
        name="pack_here",
    )(own, by_both, by_core, far, by_y, flags)
    ring_1 = send(here, RING)
    fars = [far] + [send(far, p) for p in (SWAP_CORE, SWAP_BOTH, SWAP_Y)]

    state = (
        jax.ShapeDtypeStruct((heads * rows, HEAD), jnp.float32),
        jax.ShapeDtypeStruct((heads * rows, 2 * HEAD), jnp.float32),
    )
    q2, m, acc = pl.pallas_call(
        functools.partial(local_kernel, rows=rows, heads=heads, n_tp=n_tp),
        in_specs=[smem, vmem, vmem],
        out_specs=[vmem] * 3,
        out_shape=(jax.ShapeDtypeStruct((heads * rows, 2 * HEAD), jnp.bfloat16),) + state,
        scratch_shapes=[pltpu.VMEM((4 * rows, 2 * HEAD), jnp.bfloat16)] * 2,
        compiler_params=params(36),
        cost_estimate=cost(4 * rows),
        name="attend_local",
    )(flags, queries, here)

    def step(name, at, groups, m, acc):
        counts = [len(group) for group in groups]
        n = sum(counts)
        return pl.pallas_call(
            functools.partial(step_kernel, rows=rows, heads=heads, at=at, counts=counts),
            in_specs=[smem] + [vmem] * (3 + n),
            out_specs=[vmem] * 2,
            out_shape=state,
            input_output_aliases={2 + n: 0, 3 + n: 1},
            scratch_shapes=[pltpu.VMEM((8 * rows, 2 * HEAD), jnp.bfloat16)] * 2,
            compiler_params=params(36),
            cost_estimate=cost(8 * rows),
            name=name,
        )(flags, q2, *groups[0], *groups[1], m, acc)

    ring_1 = after(ring_1, m)
    ring_2, other_1 = send(ring_1, RING), send(ring_1, SWAP_CORE)
    m, acc = step("attend_1", (OWN + 1, HALF), [[ring_1], fars], m, acc)
    ring_2 = after(ring_2, m)
    ring_3, other_2 = send(ring_2, RING), send(ring_2, SWAP_CORE)
    m, acc = step("attend_2", (OTHER + 1, OWN + 2), [[other_1], [ring_2]], m, acc)
    ring_3 = after(ring_3, m)
    other_3 = send(ring_3, SWAP_CORE)
    m, acc = step("attend_3", (OTHER + 2, OWN + 3), [[other_2], [ring_3]], m, acc)

    each, split = rows // n_tp, width * 9 // 16
    bf16 = functools.partial(jax.ShapeDtypeStruct, dtype=jnp.bfloat16)
    keep, give_y, *over_x = pl.pallas_call(
        functools.partial(last_kernel, rows=rows, heads=heads, n_tp=n_tp),
        in_specs=[smem] + [vmem] * 5 + [anywhere],
        out_specs=[vmem] * 6,
        out_shape=[bf16((rows // 2, split))] * 2 + [bf16((2 * each, width - split + LANES))] * X,
        scratch_shapes=[
            pltpu.VMEM((rows + STEP_ROWS, heads * HEAD), jnp.bfloat16),
            pltpu.VMEM(state[1].shape, jnp.float32),
            pltpu.VMEM(state[0].shape, jnp.float32),
            pltpu.VMEM((4 * rows, 2 * HEAD), jnp.bfloat16),
            pltpu.VMEM((4 * rows, 2 * HEAD), jnp.bfloat16),
            pltpu.VMEM(out_weight.shape, jnp.bfloat16),
            pltpu.VMEM((STEP_ROWS, width), jnp.float32),
            pltpu.SemaphoreType.DMA,
        ],
        compiler_params=params(44),
        cost_estimate=cost(4 * rows, 2 * rows * heads * HEAD * width),
        name="attend_project",
    )(flags, q2, other_3, m, acc, step_attention, out_weight)
    from_y = lax.ppermute(give_y, "tp", OVER_Y)
    from_x = [lax.ppermute(over_x[dx], "tp", over_x_pairs(dx)) for dx in (2, 1, 3)]
    f0, *give_x, mine, give = pl.pallas_call(
        middle_kernel,
        in_specs=[vmem] * 6,
        out_specs=[vmem] * 6,
        out_shape=[jax.ShapeDtypeStruct((each, split), jnp.float32)] + [bf16((each, split))] * 3
        + [jax.ShapeDtypeStruct((each, width - split + LANES), jnp.float32), bf16((each, width - split + LANES))],
        compiler_params=params(24),
        name="sum_first",
    )(keep, from_y, over_x[0], *from_x)
    given = lax.ppermute(give, "tp", OVER_Y)
    given_x = [lax.ppermute(give_x[dx - 1], "tp", over_x_pairs(dx)) for dx in (2, 1, 3)]
    prefill_out, decode_out = pl.pallas_call(
        sum_kernel,
        in_specs=[vmem] * 6,
        out_specs=[vmem] * 2,
        out_shape=[bf16((each, width)), bf16((1, width // n_tp))],
        compiler_params=params(24),
        name="sum_last",
    )(f0, *given_x, mine, given)
    return prefill_out, decode_out


def solution(mesh):
    return jax.shard_map(
        body,
        mesh=mesh,
        in_specs=(
            P("seq", "tp"),
            P("seq", "tp"),
            P("seq", "tp"),
            P("tp", None),
            P("seq", "tp"),
            P("seq", "tp"),
            P("seq", "tp"),
            P("seq", None, "tp"),
            P("seq", None, "tp"),
            P("seq"),
        ),
        out_specs=(P(("seq", "tp"), None), P("seq", "tp")),
        check_vma=False,
    )
```

```python
import functools
import math

import jax
import jax.numpy as jnp
from jax import lax
from jax.experimental import pallas as pl
from jax.experimental.pallas import tpu as pltpu
from jax.sharding import PartitionSpec as P

HEAD = 128
SCALE = HEAD ** -0.5 * math.log2(math.e)
LOW = -1e30
LANES = 128
STEP_ROWS = 16
LANES = 128
STEP_ROWS = 16
NT = (((1,), (1,)), ((), ()))
EDGES, HALF, OWN, OTHER, START = 0, 4, 4, 7, 11
Z, YH, CORE = 8, 2, 2


def seq_pairs(move):
    pairs = []
    for z in range(Z):
        for yh in range(YH):
            for c in range(CORE):
                z2, yh2, c2 = move(z, yh, c)
                pairs.append(((z * YH + yh) * CORE + c, ((z2 % Z) * YH + yh2) * CORE + c2))
    return pairs


SWAP_Y = seq_pairs(lambda z, yh, c: (z, 1 - yh, c))
SWAP_CORE = seq_pairs(lambda z, yh, c: (z, yh, 1 - c))
SWAP_BOTH = seq_pairs(lambda z, yh, c: (z, 1 - yh, 1 - c))
FAR = seq_pairs(lambda z, yh, c: (z + Z // 2 if z < Z // 2 else Z - 1 - z, yh, c))
RING = seq_pairs(lambda z, yh, c: (z + 1 if c == 0 else z - 1, yh, c))


X, YL = 4, 2
OVER_Y = [(x * YL + y, x * YL + 1 - y) for x in range(X) for y in range(YL)]


def over_x_pairs(dx):
    return [(x * YL + y, (x + dx) % X * YL + y) for x in range(X) for y in range(YL)]


def split_queries(flag_ref, q_ref, q2_ref, rows, heads, n_tp):
    each = rows // n_tp
    for i in range(n_tp):
        start = pl.multiple_of(flag_ref[START + i], each)
        for h in range(heads):
            scaled = q_ref[pl.ds(start, each), h * HEAD:(h + 1) * HEAD].astype(jnp.float32) * SCALE
            high = scaled.astype(jnp.bfloat16)
            low = (scaled - high.astype(jnp.float32)).astype(jnp.bfloat16)
            at = h * rows + i * each
            q2_ref[at:at + each, :HEAD] = high
            q2_ref[at:at + each, HEAD:] = low


def spread(sources, k2_ref, v2_ref, at, rows):
    for src in sources:
        for b in range(src.shape[0] // (2 * rows)):
            k = src[2 * b * rows:(2 * b + 1) * rows, :]
            v = src[(2 * b + 1) * rows:(2 * b + 2) * rows, :]
            k2_ref[at:at + rows, :HEAD] = k
            k2_ref[at:at + rows, HEAD:] = k
            v2_ref[at:at + rows, :HEAD] = v
            v2_ref[at:at + rows, HEAD:] = jnp.ones_like(v)
            at += rows


def attend(q2_ref, k2_ref, v2_ref, n, m_ref, acc_ref, m_out, acc_out, rows, heads, mask=None):
    first = m_ref is None
    together = heads // 2 if heads % 2 == 0 else heads

    def some_heads(i, _):
        parts = [pl.ds(pl.multiple_of((i * together + j) * rows, rows), rows) for j in range(together)]
        scores = [
            lax.dot_general(q2_ref[part, :], k2_ref[:n, :], NT, preferred_element_type=jnp.float32) for part in parts
        ]
        for part, s in zip(parts, scores):
            if mask is not None:
                s = jnp.where(mask, s, LOW)
            peak = jnp.max(s, axis=1, keepdims=True)
            if not first:
                old = m_ref[part, :1]
                peak = jnp.maximum(old, peak)
            p = jnp.exp2(s - peak).astype(jnp.bfloat16)
            mixed = jnp.dot(p, v2_ref[:n, :], preferred_element_type=jnp.float32)
            if not first:
                mixed = mixed + acc_ref[part, :] * jnp.exp2(old - peak)
            acc_out[part, :] = mixed
            m_out[part, :] = jnp.broadcast_to(peak, (rows, HEAD))
        return 0

    lax.fori_loop(0, heads // together, some_heads, 0)


def local_kernel(flag_ref, q_ref, kv_ref, q2_ref, m_ref, acc_ref, k2_ref, v2_ref, *, rows, heads, n_tp):
    split_queries(flag_ref, q_ref, q2_ref, rows, heads, n_tp)
    spread([kv_ref], k2_ref, v2_ref, 0, rows)
    each = rows // n_tp
    place = lax.broadcasted_iota(jnp.int32, (rows, rows), 0)
    row = place
    for i in range(n_tp):
        inside = jnp.logical_and(place >= i * each, place < (i + 1) * each)
        row = jnp.where(inside, place + (flag_ref[START + i] - i * each), row)
    col = lax.broadcasted_iota(jnp.int32, (rows, rows), 1)
    mask = jnp.concatenate([(row - col) >= flag_ref[EDGES + b] for b in range(4)], axis=1)
    attend(q2_ref, k2_ref, v2_ref, 4 * rows, None, None, m_ref, acc_ref, rows, heads, mask)


def attend_live(flag_ref, at, q2_ref, groups, k2_ref, v2_ref, m_in, acc_in, m_ref, acc_ref, rows, heads):
    n = 4 * rows
    live = [flag_ref[i] == 1 for i in at]
    if len(groups) == 1:
        some, one = live[0], live[0]
    else:
        some, one = jnp.logical_or(*live), jnp.logical_xor(*live)

        @pl.when(jnp.logical_and(*live))
        def _():
            spread(groups[0], k2_ref, v2_ref, 0, rows)
            spread(groups[1], k2_ref, v2_ref, n, rows)
            attend(q2_ref, k2_ref, v2_ref, 2 * n, m_in, acc_in, m_ref, acc_ref, rows, heads)

    @pl.when(one)
    def _():
        for here, group in zip(live, groups):
            @pl.when(here)
            def _():
                spread(group, k2_ref, v2_ref, 0, rows)

        attend(q2_ref, k2_ref, v2_ref, n, m_in, acc_in, m_ref, acc_ref, rows, heads)

    @pl.when(jnp.logical_not(some))
    def _():
        m_ref[...] = m_in[...]
        acc_ref[...] = acc_in[...]


def step_kernel(flag_ref, q2_ref, *refs, rows, heads, at, counts, passes):
    groups = [refs[:counts[0]], refs[counts[0]:sum(counts)]]
    if passes is None:
        m_in, acc_in, m_ref, acc_ref, k2_ref, v2_ref = refs[sum(counts):]
    else:
        m_in, acc_in, m_ref, acc_ref, pass_ref, k2_ref, v2_ref = refs[sum(counts):]
        pass_ref[...] = groups[passes][0][...]
    attend_live(flag_ref, at, q2_ref, groups, k2_ref, v2_ref, m_in, acc_in, m_ref, acc_ref, rows, heads)


def last_kernel(flag_ref, q2_ref, other_ref, m_in, acc_in, step_ref, w_hbm, keep_ref, send_ref, g0_ref, g1_ref, g2_ref,
                g3_ref, att_ref, acc_ref, m_ref, k2_ref, v2_ref, w_ref, token_ref, w_sem, *, rows, heads, n_tp):
    w_copy = pltpu.make_async_copy(w_hbm, w_ref, w_sem)
    w_copy.start()
    attend_live(flag_ref, (OTHER + 3,), q2_ref, [[other_ref]], k2_ref, v2_ref,
                m_in, acc_in, m_ref, acc_ref, rows, heads)
    for h in range(heads):
        cols = slice(h * HEAD, (h + 1) * HEAD)
        acc = acc_ref[h * rows:(h + 1) * rows, :]
        att_ref[:rows, cols] = (acc[:, :HEAD] / acc[:, HEAD:]).astype(jnp.bfloat16)
        att_ref[rows:, cols] = jnp.broadcast_to(step_ref[h:h + 1, :], (STEP_ROWS, HEAD)).astype(jnp.bfloat16)
    w_copy.wait()
    each, wide, split, piece = rows // n_tp, w_ref.shape[1] // n_tp, keep_ref.shape[1], 256
    g_refs = (g0_ref, g1_ref, g2_ref, g3_ref)
    for c in range(0, w_ref.shape[1], piece):
        part = jnp.dot(att_ref[...], w_ref[:, c:c + piece], preferred_element_type=jnp.float32)
        token_ref[:, c:c + piece] = part[rows:, :]
        part = part.astype(jnp.bfloat16)
        if c < split:
            keep_ref[:, c:c + piece] = part[:rows // 2, :]
            send_ref[:, c:c + piece] = part[rows // 2:rows, :]
        else:
            cols = slice(c - split, c - split + piece)
            for dx, g_ref in enumerate(g_refs):
                g_ref[:each, cols] = part[dx * each:(dx + 1) * each, :]
                g_ref[each:2 * each, cols] = part[rows // 2 + dx * each:rows // 2 + (dx + 1) * each, :]
    line = lax.broadcasted_iota(jnp.int32, (each, LANES), 0)
    for i in range(n_tp):
        dy, dx = divmod(i, X)
        start = pl.multiple_of(flag_ref[START + i] * (wide // each), wide)
        tile = jnp.zeros((each, LANES), jnp.float32)
        for j in range(wide // LANES):
            tile = jnp.where(line == j, token_ref[:1, pl.ds(start + j * LANES, LANES)], tile)
        g_refs[dx][dy * each:(dy + 1) * each, -LANES:] = tile.astype(jnp.bfloat16)


def middle_kernel(keep_ref, recv_ref, g0_ref, g1_ref, g2_ref, g3_ref, f0_ref, f1_ref, f2_ref, f3_ref, mine_ref, give_ref):
    each = f0_ref.shape[0]
    for dx, f_ref in enumerate((f0_ref, f1_ref, f2_ref, f3_ref)):
        part = slice(dx * each, (dx + 1) * each)
        total = keep_ref[part, :].astype(jnp.float32) + recv_ref[part, :].astype(jnp.float32)
        f_ref[...] = total.astype(f_ref.dtype)
    for at, ref in ((0, mine_ref), (each, give_ref)):
        total = g0_ref[at:at + each, :].astype(jnp.float32)
        for g_ref in (g1_ref, g2_ref, g3_ref):
            total = total + g_ref[at:at + each, :].astype(jnp.float32)
        ref[...] = total.astype(ref.dtype)


def sum_kernel(f0_ref, f1_ref, f2_ref, f3_ref, mine_ref, give_ref, out_ref, step_ref):
    split, rest = f0_ref.shape[1], mine_ref.shape[1] - LANES
    total = f0_ref[...]
    for ref in (f1_ref, f2_ref, f3_ref):
        total = total + ref[...].astype(jnp.float32)
    out_ref[:, :split] = total.astype(jnp.bfloat16)
    total = mine_ref[...] + give_ref[...].astype(jnp.float32)
    out_ref[:, split:] = total[:, :rest].astype(jnp.bfloat16)
    for j in range(step_ref.shape[1] // LANES):
        step_ref[:, j * LANES:(j + 1) * LANES] = total[j:j + 1, rest:].astype(jnp.bfloat16)


def decode_kernel(len_ref, q_ref, nk_ref, nv_ref, k_hbm, v_hbm, out_ref, k_ref, v_ref, k_sem, v_sem, *, heads):
    k_copy = pltpu.make_async_copy(k_hbm.at[0], k_ref, k_sem)
    v_copy = pltpu.make_async_copy(v_hbm.at[0], v_ref, v_sem)
    k_copy.start()
    v_copy.start()
    query = jnp.concatenate([q_ref[:, h * HEAD:(h + 1) * HEAD] for h in range(heads)], axis=0).astype(jnp.float32)
    scaled = query * SCALE
    high = scaled.astype(jnp.bfloat16)
    low = (scaled - high.astype(jnp.float32)).astype(jnp.bfloat16)
    both = jnp.concatenate([high, low], axis=0)
    own = jnp.sum(query * nk_ref[...].astype(jnp.float32), axis=1, keepdims=True) * SCALE
    k_copy.wait()
    s = lax.dot_general(both, k_ref[...], NT, preferred_element_type=jnp.float32)
    s = s[:heads, :] + s[heads:, :]
    slot = lax.broadcasted_iota(jnp.int32, s.shape, 1)
    s = jnp.where(slot < len_ref[0], s, LOW)
    peak = jnp.maximum(jnp.max(s, axis=1, keepdims=True), own)
    p = jnp.exp2(s - peak)
    own = jnp.exp2(own - peak)
    total = jnp.sum(p, axis=1, keepdims=True) + own
    v_copy.wait()
    mixed = jnp.dot(p.astype(jnp.bfloat16), v_ref[...], preferred_element_type=jnp.float32)
    mixed = mixed + own.astype(jnp.bfloat16).astype(jnp.float32) * nv_ref[...].astype(jnp.float32)
    out_ref[...] = mixed / total


def pack_own_kernel(k_hbm, v_hbm, out_ref, k_sem, v_sem):
    rows = k_hbm.shape[0]
    k_copy = pltpu.make_async_copy(k_hbm, out_ref.at[pl.ds(0, rows)], k_sem)
    v_copy = pltpu.make_async_copy(v_hbm, out_ref.at[pl.ds(rows, rows)], v_sem)
    k_copy.start()
    v_copy.start()
    k_copy.wait()
    v_copy.wait()


def pack_here_kernel(own_ref, both_ref, core_ref, far_ref, y_ref, _, here_ref, far_out_ref):
    at = 0
    for ref in (own_ref, y_ref, core_ref, both_ref):
        here_ref[at:at + ref.shape[0], :] = ref[...]
        at += ref.shape[0]
    far_out_ref[...] = far_ref[...]


def gate_kernel(*_):
    pass


def after(block, *others):
    anywhere = pl.BlockSpec(memory_space=pl.ANY)
    return pl.pallas_call(
        gate_kernel,
        in_specs=[anywhere] * (1 + len(others)),
        out_specs=anywhere,
        out_shape=jax.ShapeDtypeStruct(block.shape, block.dtype),
        input_output_aliases={0: 0},
        compiler_params=pltpu.CompilerParams(vmem_limit_bytes=2**20),
        name="gate",
    )(block, *others)


def body(queries, keys, values, out_weight, step_queries, new_keys, new_values, key_cache, value_cache, cache_lens):
    rows = queries.shape[0]
    heads = queries.shape[1] // HEAD
    n_tp = lax.axis_size("tp")
    width = out_weight.shape[1]
    seq = lax.axis_index("seq")
    z, yh, core = seq // (YH * CORE), seq // CORE % YH, seq % CORE
    vmem = pl.BlockSpec(memory_space=pltpu.VMEM)
    smem = pl.BlockSpec(memory_space=pltpu.SMEM)
    anywhere = pl.BlockSpec(memory_space=pl.ANY)

    def params(mib):
        return pltpu.CompilerParams(vmem_limit_bytes=mib * 2**20)

    def cost(keys_seen, more_flops=0):
        return pl.CostEstimate(
            flops=4 * heads * rows * keys_seen * 256 + more_flops,
            bytes_accessed=2**20,
            transcendentals=heads * rows * keys_seen,
        )

    def send(block, pairs):
        return lax.ppermute(block, "seq", pairs)

    own_ring = [jnp.where(core == 0, z >= k, z + k >= Z) for k in range(1, 4)]
    other_ring = [jnp.where(core == 0, z + k >= Z, z >= k) for k in range(1, 4)]
    edges = [jnp.int32(0)] + [jnp.where(c == 1, -rows, rows) for c in (yh, core, yh)]
    tp = lax.axis_index("tp")
    starts = [
        ((tp // YL + dx) % X * YL + (tp % YL + dy) % YL) * (rows // n_tp) for dy in range(YL) for dx in range(X)
    ]
    flags = jnp.stack([x.astype(jnp.int32) for x in edges + [z >= Z // 2] + own_ring + other_ring + starts])

    own = pl.pallas_call(
        pack_own_kernel,
        in_specs=[anywhere] * 2,
        out_specs=vmem,
        out_shape=jax.ShapeDtypeStruct((2 * rows, HEAD), jnp.bfloat16),
        scratch_shapes=[pltpu.SemaphoreType.DMA] * 2,
        compiler_params=params(60),
        name="pack_own",
    )(keys, values)
    by_core, far, by_y = (send(own, p) for p in (SWAP_CORE, FAR, SWAP_Y))
    step_attention = pl.pallas_call(
        functools.partial(decode_kernel, heads=heads),
        in_specs=[smem] + [vmem] * 3 + [anywhere] * 2,
        out_specs=vmem,
        out_shape=jax.ShapeDtypeStruct((heads, HEAD), jnp.float32),
        scratch_shapes=[pltpu.VMEM(key_cache.shape[1:], jnp.bfloat16)] * 2 + [pltpu.SemaphoreType.DMA] * 2,
        compiler_params=params(60),
        cost_estimate=pl.CostEstimate(flops=10**9, bytes_accessed=2 * 2**20, transcendentals=heads * key_cache.shape[1]),
        name="decode",
    )(cache_lens, step_queries, new_keys, new_values, key_cache, value_cache)
    by_y = after(by_y, step_attention)
    by_both = send(by_y, SWAP_CORE)
    here, far = pl.pallas_call(
        pack_here_kernel,
        in_specs=[vmem] * 5 + [smem],
        out_specs=[vmem] * 2,
        out_shape=[jax.ShapeDtypeStruct((n * rows, HEAD), jnp.bfloat16) for n in (8, 2)],
        compiler_params=params(4),
        name="pack_here",
    )(own, by_both, by_core, far, by_y, flags)
    ring_1 = send(here, RING)
    fars = [far] + [send(far, p) for p in (SWAP_CORE, SWAP_BOTH, SWAP_Y)]

    state = (
        jax.ShapeDtypeStruct((heads * rows, HEAD), jnp.float32),
        jax.ShapeDtypeStruct((heads * rows, 2 * HEAD), jnp.float32),
    )
    q2, m, acc = pl.pallas_call(
        functools.partial(local_kernel, rows=rows, heads=heads, n_tp=n_tp),
        in_specs=[smem, vmem, vmem],
        out_specs=[vmem] * 3,
        out_shape=(jax.ShapeDtypeStruct((heads * rows, 2 * HEAD), jnp.bfloat16),) + state,
        scratch_shapes=[pltpu.VMEM((4 * rows, 2 * HEAD), jnp.bfloat16)] * 2,
        compiler_params=params(36),
        cost_estimate=cost(4 * rows),
        name="attend_local",
    )(flags, queries, here)

    def step(name, at, groups, m, acc, passes=None):
        counts = [len(group) for group in groups]
        n = sum(counts)
        passed = () if passes is None else (jax.ShapeDtypeStruct(groups[passes][0].shape, jnp.bfloat16),)
        return pl.pallas_call(
            functools.partial(step_kernel, rows=rows, heads=heads, at=at, counts=counts, passes=passes),
            in_specs=[smem] + [vmem] * (3 + n),
            out_specs=[vmem] * (2 if passes is None else 3),
            out_shape=state + passed,
            input_output_aliases={2 + n: 0, 3 + n: 1},
            scratch_shapes=[pltpu.VMEM((8 * rows, 2 * HEAD), jnp.bfloat16)] * 2,
            compiler_params=params(36),
            cost_estimate=cost(8 * rows),
            name=name,
        )(flags, q2, *groups[0], *groups[1], m, acc)

    ring_1 = after(ring_1, m)
    ring_2 = send(ring_1, RING)
    m, acc, other_1 = step("attend_1", (OWN + 1, HALF), [[ring_1], fars], m, acc, passes=0)
    other_1 = send(other_1, SWAP_CORE)
    ring_2 = after(ring_2, m)
    ring_3 = send(ring_2, RING)
    m, acc, other_2 = step("attend_2", (OTHER + 1, OWN + 2), [[other_1], [ring_2]], m, acc, passes=1)
    other_2 = send(other_2, SWAP_CORE)
    ring_3 = after(ring_3, m)
    other_3 = send(ring_3, SWAP_CORE)
    m, acc = step("attend_3", (OTHER + 2, OWN + 3), [[other_2], [ring_3]], m, acc)

    each, split = rows // n_tp, width * 9 // 16
    bf16 = functools.partial(jax.ShapeDtypeStruct, dtype=jnp.bfloat16)
    keep, give_y, *over_x = pl.pallas_call(
        functools.partial(last_kernel, rows=rows, heads=heads, n_tp=n_tp),
        in_specs=[smem] + [vmem] * 5 + [anywhere],
        out_specs=[vmem] * 6,
        out_shape=[bf16((rows // 2, split))] * 2 + [bf16((2 * each, width - split + LANES))] * X,
        scratch_shapes=[
            pltpu.VMEM((rows + STEP_ROWS, heads * HEAD), jnp.bfloat16),
            pltpu.VMEM(state[1].shape, jnp.float32),
            pltpu.VMEM(state[0].shape, jnp.float32),
            pltpu.VMEM((4 * rows, 2 * HEAD), jnp.bfloat16),
            pltpu.VMEM((4 * rows, 2 * HEAD), jnp.bfloat16),
            pltpu.VMEM(out_weight.shape, jnp.bfloat16),
            pltpu.VMEM((STEP_ROWS, width), jnp.float32),
            pltpu.SemaphoreType.DMA,
        ],
        compiler_params=params(44),
        cost_estimate=cost(4 * rows, 2 * rows * heads * HEAD * width),
        name="attend_project",
    )(flags, q2, other_3, m, acc, step_attention, out_weight)
    from_y = lax.ppermute(give_y, "tp", OVER_Y)
    from_x = [lax.ppermute(over_x[dx], "tp", over_x_pairs(dx)) for dx in (2, 1, 3)]
    f0, *give_x, mine, give = pl.pallas_call(
        middle_kernel,
        in_specs=[vmem] * 6,
        out_specs=[vmem] * 6,
        out_shape=[jax.ShapeDtypeStruct((each, split), jnp.float32)] + [bf16((each, split))] * 3
        + [jax.ShapeDtypeStruct((each, width - split + LANES), jnp.float32), bf16((each, width - split + LANES))],
        compiler_params=params(24),
        name="sum_first",
    )(keep, from_y, over_x[0], *from_x)
    given = lax.ppermute(give, "tp", OVER_Y)
    given_x = [lax.ppermute(give_x[dx - 1], "tp", over_x_pairs(dx)) for dx in (2, 1, 3)]
    prefill_out, decode_out = pl.pallas_call(
        sum_kernel,
        in_specs=[vmem] * 6,
        out_specs=[vmem] * 2,
        out_shape=[bf16((each, width)), bf16((1, width // n_tp))],
        compiler_params=params(24),
        name="sum_last",
    )(f0, *given_x, mine, given)
    return prefill_out, decode_out


def solution(mesh):
    return jax.shard_map(
        body,
        mesh=mesh,
        in_specs=(
            P("seq", "tp"),
            P("seq", "tp"),
            P("seq", "tp"),
            P("tp", None),
            P("seq", "tp"),
            P("seq", "tp"),
            P("seq", "tp"),
            P("seq", None, "tp"),
            P("seq", None, "tp"),
            P("seq"),
        ),
        out_specs=(P(("seq", "tp"), None), P("seq", "tp")),
        check_vma=False,
    )
```

```python
import functools
import math

import jax
import jax.numpy as jnp
from jax import lax
from jax.experimental import pallas as pl
from jax.experimental.pallas import tpu as pltpu
from jax.sharding import PartitionSpec as P

HEAD = 128
SCALE = HEAD ** -0.5 * math.log2(math.e)
LOW = -1e30
LANES = 128
STEP_ROWS = 16
LANES = 128
STEP_ROWS = 16
NT = (((1,), (1,)), ((), ()))
EDGES, HALF, OWN, OTHER, START = 0, 4, 4, 7, 11
Z, YH, CORE = 8, 2, 2


def seq_pairs(move):
    pairs = []
    for z in range(Z):
        for yh in range(YH):
            for c in range(CORE):
                z2, yh2, c2 = move(z, yh, c)
                pairs.append(((z * YH + yh) * CORE + c, ((z2 % Z) * YH + yh2) * CORE + c2))
    return pairs


SWAP_Y = seq_pairs(lambda z, yh, c: (z, 1 - yh, c))
SWAP_CORE = seq_pairs(lambda z, yh, c: (z, yh, 1 - c))
SWAP_BOTH = seq_pairs(lambda z, yh, c: (z, 1 - yh, 1 - c))
FAR = seq_pairs(lambda z, yh, c: (z + Z // 2 if z < Z // 2 else Z - 1 - z, yh, c))
RING = seq_pairs(lambda z, yh, c: (z + 1 if c == 0 else z - 1, yh, c))


X, YL = 4, 2
OVER_Y = [(x * YL + y, x * YL + 1 - y) for x in range(X) for y in range(YL)]


def over_x_pairs(dx):
    return [(x * YL + y, (x + dx) % X * YL + y) for x in range(X) for y in range(YL)]


def split_queries(flag_ref, q_ref, q2_ref, rows, heads, n_tp):
    each = rows // n_tp
    for i in range(n_tp):
        start = pl.multiple_of(flag_ref[START + i], each)
        for h in range(heads):
            scaled = q_ref[pl.ds(start, each), h * HEAD:(h + 1) * HEAD].astype(jnp.float32) * SCALE
            high = scaled.astype(jnp.bfloat16)
            low = (scaled - high.astype(jnp.float32)).astype(jnp.bfloat16)
            at = h * rows + i * each
            q2_ref[at:at + each, :HEAD] = high
            q2_ref[at:at + each, HEAD:] = low


def spread(sources, k2_ref, v2_ref, at, rows):
    for src in sources:
        for b in range(src.shape[0] // (2 * rows)):
            k = src[2 * b * rows:(2 * b + 1) * rows, :]
            v = src[(2 * b + 1) * rows:(2 * b + 2) * rows, :]
            k2_ref[at:at + rows, :HEAD] = k
            k2_ref[at:at + rows, HEAD:] = k
            v2_ref[at:at + rows, :HEAD] = v
            v2_ref[at:at + rows, HEAD:] = jnp.ones_like(v)
            at += rows


def attend(q2_ref, k2_ref, v2_ref, n, m_ref, acc_ref, m_out, acc_out, rows, heads, mask=None):
    first = m_ref is None
    together = heads // 2 if heads % 2 == 0 else heads

    def some_heads(i, _):
        parts = [pl.ds(pl.multiple_of((i * together + j) * rows, rows), rows) for j in range(together)]
        scores = [
            lax.dot_general(q2_ref[part, :], k2_ref[:n, :], NT, preferred_element_type=jnp.float32) for part in parts
        ]
        for part, s in zip(parts, scores):
            if mask is not None:
                s = jnp.where(mask, s, LOW)
            peak = jnp.max(s, axis=1, keepdims=True)
            if not first:
                old = m_ref[part, :1]
                peak = jnp.maximum(old, peak)
            p = jnp.exp2(s - peak).astype(jnp.bfloat16)
            mixed = jnp.dot(p, v2_ref[:n, :], preferred_element_type=jnp.float32)
            if not first:
                mixed = mixed + acc_ref[part, :] * jnp.exp2(old - peak)
            acc_out[part, :] = mixed
            m_out[part, :] = jnp.broadcast_to(peak, (rows, HEAD))
        return 0

    lax.fori_loop(0, heads // together, some_heads, 0)


def local_kernel(flag_ref, q_ref, kv_ref, q2_ref, m_ref, acc_ref, k2_ref, v2_ref, *, rows, heads, n_tp):
    split_queries(flag_ref, q_ref, q2_ref, rows, heads, n_tp)
    spread([kv_ref], k2_ref, v2_ref, 0, rows)
    each = rows // n_tp
    place = lax.broadcasted_iota(jnp.int32, (rows, rows), 0)
    row = place
    for i in range(n_tp):
        inside = jnp.logical_and(place >= i * each, place < (i + 1) * each)
        row = jnp.where(inside, place + (flag_ref[START + i] - i * each), row)
    col = lax.broadcasted_iota(jnp.int32, (rows, rows), 1)
    mask = jnp.concatenate([(row - col) >= flag_ref[EDGES + b] for b in range(4)], axis=1)
    attend(q2_ref, k2_ref, v2_ref, 4 * rows, None, None, m_ref, acc_ref, rows, heads, mask)


def attend_live(flag_ref, at, q2_ref, groups, k2_ref, v2_ref, m_in, acc_in, m_ref, acc_ref, rows, heads):
    n = 4 * rows
    live = [flag_ref[i] == 1 for i in at]
    if len(groups) == 1:
        some, one = live[0], live[0]
    else:
        some, one = jnp.logical_or(*live), jnp.logical_xor(*live)

        @pl.when(jnp.logical_and(*live))
        def _():
            spread(groups[0], k2_ref, v2_ref, 0, rows)
            spread(groups[1], k2_ref, v2_ref, n, rows)
            attend(q2_ref, k2_ref, v2_ref, 2 * n, m_in, acc_in, m_ref, acc_ref, rows, heads)

    @pl.when(one)
    def _():
        for here, group in zip(live, groups):
            @pl.when(here)
            def _():
                spread(group, k2_ref, v2_ref, 0, rows)

        attend(q2_ref, k2_ref, v2_ref, n, m_in, acc_in, m_ref, acc_ref, rows, heads)

    @pl.when(jnp.logical_not(some))
    def _():
        m_ref[...] = m_in[...]
        acc_ref[...] = acc_in[...]


def step_kernel(flag_ref, q2_ref, *refs, rows, heads, at, counts):
    groups = [refs[:counts[0]], refs[counts[0]:sum(counts)]]
    m_in, acc_in, m_ref, acc_ref, k2_ref, v2_ref = refs[sum(counts):]
    attend_live(flag_ref, at, q2_ref, groups, k2_ref, v2_ref, m_in, acc_in, m_ref, acc_ref, rows, heads)


def last_kernel(flag_ref, q2_ref, other_ref, m_in, acc_in, step_ref, w_hbm, keep_ref, send_ref, g0_ref, g1_ref, g2_ref,
                g3_ref, att_ref, acc_ref, m_ref, k2_ref, v2_ref, w_ref, token_ref, w_sem, *, rows, heads, n_tp):
    w_copy = pltpu.make_async_copy(w_hbm, w_ref, w_sem)
    w_copy.start()
    attend_live(flag_ref, (OTHER + 3,), q2_ref, [[other_ref]], k2_ref, v2_ref,
                m_in, acc_in, m_ref, acc_ref, rows, heads)
    for h in range(heads):
        cols = slice(h * HEAD, (h + 1) * HEAD)
        acc = acc_ref[h * rows:(h + 1) * rows, :]
        att_ref[:rows, cols] = (acc[:, :HEAD] / acc[:, HEAD:]).astype(jnp.bfloat16)
        att_ref[rows:, cols] = jnp.broadcast_to(step_ref[h:h + 1, :], (STEP_ROWS, HEAD)).astype(jnp.bfloat16)
    w_copy.wait()
    each, wide, split, piece = rows // n_tp, w_ref.shape[1] // n_tp, keep_ref.shape[1], 256
    g_refs = (g0_ref, g1_ref, g2_ref, g3_ref)
    for c in range(0, w_ref.shape[1], piece):
        part = jnp.dot(att_ref[...], w_ref[:, c:c + piece], preferred_element_type=jnp.float32)
        token_ref[:, c:c + piece] = part[rows:, :]
        part = part.astype(jnp.bfloat16)
        if c < split:
            keep_ref[:, c:c + piece] = part[:rows // 2, :]
            send_ref[:, c:c + piece] = part[rows // 2:rows, :]
        else:
            cols = slice(c - split, c - split + piece)
            for dx, g_ref in enumerate(g_refs):
                g_ref[:each, cols] = part[dx * each:(dx + 1) * each, :]
                g_ref[each:2 * each, cols] = part[rows // 2 + dx * each:rows // 2 + (dx + 1) * each, :]
    line = lax.broadcasted_iota(jnp.int32, (each, LANES), 0)
    for i in range(n_tp):
        dy, dx = divmod(i, X)
        start = pl.multiple_of(flag_ref[START + i] * (wide // each), wide)
        tile = jnp.zeros((each, LANES), jnp.float32)
        for j in range(wide // LANES):
            tile = jnp.where(line == j, token_ref[:1, pl.ds(start + j * LANES, LANES)], tile)
        g_refs[dx][dy * each:(dy + 1) * each, -LANES:] = tile.astype(jnp.bfloat16)


def middle_kernel(keep_ref, recv_ref, g0_ref, g1_ref, g2_ref, g3_ref, f0_ref, f1_ref, f2_ref, f3_ref, mine_ref, give_ref):
    each = f0_ref.shape[0]
    for dx, f_ref in enumerate((f0_ref, f1_ref, f2_ref, f3_ref)):
        part = slice(dx * each, (dx + 1) * each)
        total = keep_ref[part, :].astype(jnp.float32) + recv_ref[part, :].astype(jnp.float32)
        f_ref[...] = total.astype(f_ref.dtype)
    for at, ref in ((0, mine_ref), (each, give_ref)):
        total = g0_ref[at:at + each, :].astype(jnp.float32)
        for g_ref in (g1_ref, g2_ref, g3_ref):
            total = total + g_ref[at:at + each, :].astype(jnp.float32)
        ref[...] = total.astype(ref.dtype)


def sum_kernel(f0_ref, f1_ref, f2_ref, f3_ref, mine_ref, give_ref, out_ref, step_ref):
    split, rest = f0_ref.shape[1], mine_ref.shape[1] - LANES
    total = f0_ref[...]
    for ref in (f1_ref, f2_ref, f3_ref):
        total = total + ref[...].astype(jnp.float32)
    out_ref[:, :split] = total.astype(jnp.bfloat16)
    total = mine_ref[...] + give_ref[...].astype(jnp.float32)
    out_ref[:, split:] = total[:, :rest].astype(jnp.bfloat16)
    for j in range(step_ref.shape[1] // LANES):
        step_ref[:, j * LANES:(j + 1) * LANES] = total[j:j + 1, rest:].astype(jnp.bfloat16)


def decode_kernel(len_ref, q_ref, nk_ref, nv_ref, k_hbm, v_hbm, out_ref, k_ref, v_ref, k_sem, v_sem, *, heads):
    k_copy = pltpu.make_async_copy(k_hbm.at[0], k_ref, k_sem)
    v_copy = pltpu.make_async_copy(v_hbm.at[0], v_ref, v_sem)
    k_copy.start()
    v_copy.start()
    query = jnp.concatenate([q_ref[:, h * HEAD:(h + 1) * HEAD] for h in range(heads)], axis=0).astype(jnp.float32)
    scaled = query * SCALE
    high = scaled.astype(jnp.bfloat16)
    low = (scaled - high.astype(jnp.float32)).astype(jnp.bfloat16)
    both = jnp.concatenate([high, low], axis=0)
    own = jnp.sum(query * nk_ref[...].astype(jnp.float32), axis=1, keepdims=True) * SCALE
    k_copy.wait()
    s = lax.dot_general(both, k_ref[...], NT, preferred_element_type=jnp.float32)
    s = s[:heads, :] + s[heads:, :]
    slot = lax.broadcasted_iota(jnp.int32, s.shape, 1)
    s = jnp.where(slot < len_ref[0], s, LOW)
    peak = jnp.maximum(jnp.max(s, axis=1, keepdims=True), own)
    p = jnp.exp2(s - peak)
    own = jnp.exp2(own - peak)
    total = jnp.sum(p, axis=1, keepdims=True) + own
    v_copy.wait()
    mixed = jnp.dot(p.astype(jnp.bfloat16), v_ref[...], preferred_element_type=jnp.float32)
    mixed = mixed + own.astype(jnp.bfloat16).astype(jnp.float32) * nv_ref[...].astype(jnp.float32)
    out_ref[...] = mixed / total


def pack_own_kernel(k_hbm, v_hbm, out_ref, k_sem, v_sem):
    rows = k_hbm.shape[0]
    k_copy = pltpu.make_async_copy(k_hbm, out_ref.at[pl.ds(0, rows)], k_sem)
    v_copy = pltpu.make_async_copy(v_hbm, out_ref.at[pl.ds(rows, rows)], v_sem)
    k_copy.start()
    v_copy.start()
    k_copy.wait()
    v_copy.wait()


def pack_here_kernel(own_ref, both_ref, core_ref, far_ref, y_ref, _, here_ref, far_out_ref):
    at = 0
    for ref in (own_ref, y_ref, core_ref, both_ref):
        here_ref[at:at + ref.shape[0], :] = ref[...]
        at += ref.shape[0]
    far_out_ref[...] = far_ref[...]


def gate_kernel(*_):
    pass


def after(block, *others):
    anywhere = pl.BlockSpec(memory_space=pl.ANY)
    return pl.pallas_call(
        gate_kernel,
        in_specs=[anywhere] * (1 + len(others)),
        out_specs=anywhere,
        out_shape=jax.ShapeDtypeStruct(block.shape, block.dtype),
        input_output_aliases={0: 0},
        compiler_params=pltpu.CompilerParams(vmem_limit_bytes=2**20),
        name="gate",
    )(block, *others)


def body(queries, keys, values, out_weight, step_queries, new_keys, new_values, key_cache, value_cache, cache_lens):
    rows = queries.shape[0]
    heads = queries.shape[1] // HEAD
    n_tp = lax.axis_size("tp")
    width = out_weight.shape[1]
    seq = lax.axis_index("seq")
    z, yh, core = seq // (YH * CORE), seq // CORE % YH, seq % CORE
    vmem = pl.BlockSpec(memory_space=pltpu.VMEM)
    smem = pl.BlockSpec(memory_space=pltpu.SMEM)
    anywhere = pl.BlockSpec(memory_space=pl.ANY)

    def params(mib):
        return pltpu.CompilerParams(vmem_limit_bytes=mib * 2**20)

    def cost(keys_seen, more_flops=0):
        return pl.CostEstimate(
            flops=4 * heads * rows * keys_seen * 256 + more_flops,
            bytes_accessed=2**20,
            transcendentals=heads * rows * keys_seen,
        )

    def send(block, pairs):
        return lax.ppermute(block, "seq", pairs)

    own_ring = [jnp.where(core == 0, z >= k, z + k >= Z) for k in range(1, 4)]
    other_ring = [jnp.where(core == 0, z + k >= Z, z >= k) for k in range(1, 4)]
    edges = [jnp.int32(0)] + [jnp.where(c == 1, -rows, rows) for c in (yh, core, yh)]
    tp = lax.axis_index("tp")
    starts = [
        ((tp // YL + dx) % X * YL + (tp % YL + dy) % YL) * (rows // n_tp) for dy in range(YL) for dx in range(X)
    ]
    flags = jnp.stack([x.astype(jnp.int32) for x in edges + [z >= Z // 2] + own_ring + other_ring + starts])

    own = pl.pallas_call(
        pack_own_kernel,
        in_specs=[anywhere] * 2,
        out_specs=vmem,
        out_shape=jax.ShapeDtypeStruct((2 * rows, HEAD), jnp.bfloat16),
        scratch_shapes=[pltpu.SemaphoreType.DMA] * 2,
        compiler_params=params(60),
        name="pack_own",
    )(keys, values)
    by_core, far, by_y = (send(own, p) for p in (SWAP_CORE, FAR, SWAP_Y))
    step_attention = pl.pallas_call(
        functools.partial(decode_kernel, heads=heads),
        in_specs=[smem] + [vmem] * 3 + [anywhere] * 2,
        out_specs=vmem,
        out_shape=jax.ShapeDtypeStruct((heads, HEAD), jnp.float32),
        scratch_shapes=[pltpu.VMEM(key_cache.shape[1:], jnp.bfloat16)] * 2 + [pltpu.SemaphoreType.DMA] * 2,
        compiler_params=params(60),
        cost_estimate=pl.CostEstimate(flops=10**9, bytes_accessed=2 * 2**20, transcendentals=heads * key_cache.shape[1]),
        name="decode",
    )(cache_lens, step_queries, new_keys, new_values, key_cache, value_cache)
    far = after(far, step_attention)
    by_both = send(by_y, SWAP_CORE)
    here, far = pl.pallas_call(
        pack_here_kernel,
        in_specs=[vmem] * 5 + [smem],
        out_specs=[vmem] * 2,
        out_shape=[jax.ShapeDtypeStruct((n * rows, HEAD), jnp.bfloat16) for n in (8, 2)],
        compiler_params=params(4),
        name="pack_here",
    )(own, by_both, by_core, far, by_y, flags)
    ring_1 = send(here, RING)
    fars = [far] + [send(far, p) for p in (SWAP_CORE, SWAP_BOTH, SWAP_Y)]

    state = (
        jax.ShapeDtypeStruct((heads * rows, HEAD), jnp.float32),
        jax.ShapeDtypeStruct((heads * rows, 2 * HEAD), jnp.float32),
    )
    q2, m, acc = pl.pallas_call(
        functools.partial(local_kernel, rows=rows, heads=heads, n_tp=n_tp),
        in_specs=[smem, vmem, vmem],
        out_specs=[vmem] * 3,
        out_shape=(jax.ShapeDtypeStruct((heads * rows, 2 * HEAD), jnp.bfloat16),) + state,
        scratch_shapes=[pltpu.VMEM((4 * rows, 2 * HEAD), jnp.bfloat16)] * 2,
        compiler_params=params(36),
        cost_estimate=cost(4 * rows),
        name="attend_local",
    )(flags, queries, here)

    def step(name, at, groups, m, acc):
        counts = [len(group) for group in groups]
        n = sum(counts)
        return pl.pallas_call(
            functools.partial(step_kernel, rows=rows, heads=heads, at=at, counts=counts),
            in_specs=[smem] + [vmem] * (3 + n),
            out_specs=[vmem] * 2,
            out_shape=state,
            input_output_aliases={2 + n: 0, 3 + n: 1},
            scratch_shapes=[pltpu.VMEM((8 * rows, 2 * HEAD), jnp.bfloat16)] * 2,
            compiler_params=params(36),
            cost_estimate=cost(8 * rows),
            name=name,
        )(flags, q2, *groups[0], *groups[1], m, acc)

    ring_1 = after(ring_1, m)
    ring_2, other_1 = send(ring_1, RING), send(ring_1, SWAP_CORE)
    m, acc = step("attend_1", (OWN + 1, HALF), [[ring_1], fars], m, acc)
    ring_2 = after(ring_2, m)
    ring_3, other_2 = send(ring_2, RING), send(ring_2, SWAP_CORE)
    m, acc = step("attend_2", (OTHER + 1, OWN + 2), [[other_1], [ring_2]], m, acc)
    ring_3 = after(ring_3, m)
    other_3 = send(ring_3, SWAP_CORE)
    m, acc = step("attend_3", (OTHER + 2, OWN + 3), [[other_2], [ring_3]], m, acc)

    each, split = rows // n_tp, width * 9 // 16
    bf16 = functools.partial(jax.ShapeDtypeStruct, dtype=jnp.bfloat16)
    keep, give_y, *over_x = pl.pallas_call(
        functools.partial(last_kernel, rows=rows, heads=heads, n_tp=n_tp),
        in_specs=[smem] + [vmem] * 5 + [anywhere],
        out_specs=[vmem] * 6,
        out_shape=[bf16((rows // 2, split))] * 2 + [bf16((2 * each, width - split + LANES))] * X,
        scratch_shapes=[
            pltpu.VMEM((rows + STEP_ROWS, heads * HEAD), jnp.bfloat16),
            pltpu.VMEM(state[1].shape, jnp.float32),
            pltpu.VMEM(state[0].shape, jnp.float32),
            pltpu.VMEM((4 * rows, 2 * HEAD), jnp.bfloat16),
            pltpu.VMEM((4 * rows, 2 * HEAD), jnp.bfloat16),
            pltpu.VMEM(out_weight.shape, jnp.bfloat16),
            pltpu.VMEM((STEP_ROWS, width), jnp.float32),
            pltpu.SemaphoreType.DMA,
        ],
        compiler_params=params(44),
        cost_estimate=cost(4 * rows, 2 * rows * heads * HEAD * width),
        name="attend_project",
    )(flags, q2, other_3, m, acc, step_attention, out_weight)
    from_y = lax.ppermute(give_y, "tp", OVER_Y)
    from_x = [lax.ppermute(over_x[dx], "tp", over_x_pairs(dx)) for dx in (2, 1, 3)]
    f0, *give_x, mine, give = pl.pallas_call(
        middle_kernel,
        in_specs=[vmem] * 6,
        out_specs=[vmem] * 6,
        out_shape=[jax.ShapeDtypeStruct((each, split), jnp.float32)] + [bf16((each, split))] * 3
        + [jax.ShapeDtypeStruct((each, width - split + LANES), jnp.float32), bf16((each, width - split + LANES))],
        compiler_params=params(24),
        name="sum_first",
    )(keep, from_y, over_x[0], *from_x)
    given = lax.ppermute(give, "tp", OVER_Y)
    given_x = [lax.ppermute(give_x[dx - 1], "tp", over_x_pairs(dx)) for dx in (2, 1, 3)]
    prefill_out, decode_out = pl.pallas_call(
        sum_kernel,
        in_specs=[vmem] * 6,
        out_specs=[vmem] * 2,
        out_shape=[bf16((each, width)), bf16((1, width // n_tp))],
        compiler_params=params(24),
        name="sum_last",
    )(f0, *given_x, mine, given)
    return prefill_out, decode_out


def solution(mesh):
    return jax.shard_map(
        body,
        mesh=mesh,
        in_specs=(
            P("seq", "tp"),
            P("seq", "tp"),
            P("seq", "tp"),
            P("tp", None),
            P("seq", "tp"),
            P("seq", "tp"),
            P("seq", "tp"),
            P("seq", None, "tp"),
            P("seq", None, "tp"),
            P("seq"),
        ),
        out_specs=(P(("seq", "tp"), None), P("seq", "tp")),
        check_vma=False,
    )
```
